512 devices in a mesh: slab: 128 (over y, z, core), grp: 4 (over x).
Axes of the slice: x: 4, y: 4, z: 16, core: 2. Of those that a mesh axis runs over, the one named last changes fastest.
Arguments:
- pencils: float32 [256, 256, 512], P('slab', 'grp'), may hold values from -6 to 6
- send_map: int32 [128, 4, 128, 16], P('slab', 'grp'), may hold values from -1 to 511, as said below
- interp_index: int32 [2, 128, 8, 256], P(None, 'slab', None, 'grp'), may hold values from 0 to 2047, as said below
- interp_frac: float32 [128, 8, 256], P('slab', None, 'grp'), may hold values from 0 to 1
- ori_count: int32 [128], P('slab'), may hold values from 1 to 8, as said below
- spectra: bfloat16 [1024, 256, 512], P('slab', 'grp'), may hold values from -6 to 6
- class_ids: int32 [1024], P('slab'), may hold values from 0 to 15
- ctf_table: bfloat16 [16, 256, 256], P(None, 'grp'), may hold values from -1 to 1
Outputs:
- scores: float32 [1024, 512], P('slab', 'grp')
The draws below stay inside these ranges and needn't reach their ends.
Inputs may be any that keep to these rules, and one draw needn't show every extreme that they name: `send_map`: slots with index 16 or more are never used; for every row group and owner, the used slots of one source come first, at least one, and one source fills all 16. `interp_index`: every entry names a slot that send_map fills for that owner and row group. `ori_count`: some owner lists 8 orientations.
All inputs are finite; a program needn't handle non-finite values.
Results may differ from the reference program's by a relative error of at most 0.005.
Values may be sent and summed in bfloat16 or wider, within the bound.
No kernel may reach another device: no remote copies, remote signals or barrier semaphores. Data moves between devices by JAX's collectives and lax.ppermute only.
A program may use at most 64 MiB of HBM per device.

```python
import math
import jax
import jax.numpy as jnp
from jax import lax

NF = 256
CAP = 16
ORI_MAX = 8
TSIDE = 8
CLASSES = 16
PART_DEV = 8
PARTICLES = 1024
SLAB_ROWS = 512
SLOTS = 2048
TRANS = 64
N_SLAB = 128
N_GRP = 4


def slot_counts(key):
    key_fill = jax.random.fold_in(key, 101)
    key_hot = jax.random.fold_in(key, 102)
    filled = jax.random.randint(key_fill, (N_SLAB, N_GRP, N_SLAB), 1, CAP + 1)
    hottest = jax.random.randint(key_hot, (1, N_GRP, N_SLAB), 0, N_SLAB)
    sources = jnp.arange(N_SLAB, dtype=jnp.int32)[:, None, None]
    return jnp.where(sources == hottest, CAP, filled)


def draw_send_map(key, part):
    counts = slot_counts(key)
    key = jax.random.fold_in(key, 3)
    picks = jax.random.randint(key, (N_SLAB, N_GRP, N_SLAB, CAP), 0, SLAB_ROWS)
    slot_ids = jnp.arange(CAP, dtype=jnp.int32)
    return jnp.where(slot_ids < counts[..., None], picks, -1).astype(jnp.int32)


def draw_interp_index(key, part):
    counts = slot_counts(key)
    key = jax.random.fold_in(key, 5)
    key_source = jax.random.fold_in(key, 1)
    key_slot = jax.random.fold_in(key, 2)
    shape = (2, N_SLAB, ORI_MAX, NF)
    sources = jax.random.randint(key_source, shape, 0, N_SLAB)
    row_groups = jnp.broadcast_to((jnp.arange(NF, dtype=jnp.int32) // (NF // N_GRP))[None, None, None, :], shape)
    owners = jnp.broadcast_to(jnp.arange(N_SLAB, dtype=jnp.int32)[None, :, None, None], shape)
    limits = counts[sources, row_groups, owners]
    slot_ids = jax.random.randint(key_slot, shape, 0, limits)
    return (sources * CAP + slot_ids).astype(jnp.int32)


def draw_ori_count(key, part):
    key = jax.random.fold_in(key, 7)
    key_len = jax.random.fold_in(key, 1)
    key_top = jax.random.fold_in(key, 2)
    lengths = jax.random.randint(key_len, (N_SLAB,), 1, ORI_MAX + 1)
    longest = jax.random.randint(key_top, (), 0, N_SLAB)
    return jnp.where(jnp.arange(N_SLAB, dtype=jnp.int32) == longest, ORI_MAX, lengths).astype(jnp.int32)


def touch_ends(values, stream_key, smallest, top_value):
    place = [jax.random.randint(jax.random.fold_in(stream_key, axis), (), 0, length) for axis, length in enumerate(values.shape)]
    widest = values.shape.index(max(values.shape))
    beside = place[:widest] + [(place[widest] + 1) % values.shape[widest]] + place[widest + 1:]
    return values.at[tuple(place)].set(smallest).at[tuple(beside)].set(top_value)


def block_scale(own_key, shape, shards, smallest, largest):
    level = 1.0
    for axis_at, parts in shards:
        heights = jax.random.uniform(jax.random.fold_in(jax.random.fold_in(own_key, 6), axis_at), (parts,), jnp.float32, smallest / len(shards), largest / len(shards))
        level = level * jnp.repeat(jnp.exp(heights), shape[axis_at] // parts).reshape((-1,) + (1,) * (len(shape) - 1 - axis_at))
    return level


def gaussian(rng, shape, spread, reach, pieces=(), kind=jnp.bfloat16):
    values = jax.random.normal(rng, shape, jnp.float32) * spread
    if len(pieces) > 0:
        values = block_scale(rng, shape, pieces, -0.22, 0.18) * values
    return jnp.clip(values, min=-reach, max=reach).astype(kind)


def setup_inputs(seed: int = 0) -> dict:
    seeds = jax.random.split(jax.random.key(seed), 9)
    pencils = gaussian(seeds[0], (NF, NF, 2 * NF), 1.0, 6.0, ((0, 128), (1, 4)), jnp.float32)
    send_map = draw_send_map(jax.random.fold_in(seeds[8], 71), 0)
    interp_index = draw_interp_index(jax.random.fold_in(seeds[8], 71), 0)
    interp_frac = jnp.clip(1.0 * jax.random.uniform(seeds[3], (N_SLAB, ORI_MAX, NF), jnp.float32) ** block_scale(seeds[3], (N_SLAB, ORI_MAX, NF), ((0, 128), (2, 4)), -0.2, 0.2), 0.0, 1.0)
    ori_count = draw_ori_count(jax.random.fold_in(seeds[8], 71), 0)
    spectra = gaussian(seeds[5], (PARTICLES, NF, 2 * NF), 1.0, 6.0, ((0, 128), (1, 4)))
    class_ids = touch_ends(jax.random.randint(seeds[6], (PARTICLES,), 0, CLASSES), jax.random.fold_in(seeds[6], 1), 0, CLASSES - 1).astype(jnp.int32)
    ctf_table = jnp.clip(jax.random.uniform(seeds[7], (CLASSES, NF, NF), jnp.float32, -1.0, 1.0) * block_scale(seeds[7], (CLASSES, NF, NF), ((1, 4),), -0.4, 0.0), -1.0, 1.0).astype(jnp.bfloat16)
    return dict(pencils=pencils, send_map=send_map, interp_index=interp_index, interp_frac=interp_frac, ori_count=ori_count, spectra=spectra, class_ids=class_ids, ctf_table=ctf_table)


def phase_factors(first_row, row_total):
    side_ids = jnp.arange(TSIDE, dtype=jnp.int32) - TSIDE // 2
    rows_u = first_row + jnp.arange(row_total, dtype=jnp.int32)
    cols_v = jnp.arange(NF, dtype=jnp.int32)
    turns_u = side_ids[:, None] * rows_u[None, :] % NF
    turns_v = side_ids[:, None] * cols_v[None, :] % NF
    angle_u = -2.0 * math.pi / NF * turns_u.astype(jnp.float32)
    angle_v = -2.0 * math.pi / NF * turns_v.astype(jnp.float32)
    return (jnp.cos(angle_u), jnp.sin(angle_u), jnp.cos(angle_v), jnp.sin(angle_v))

def shift_score(slice_rows, weighted, factors):
    cos_u, sin_u, cos_v, sin_v = factors
    row_total = slice_rows.shape[0]
    cu = cos_u[:, None, :, None]
    su = sin_u[:, None, :, None]
    cv = cos_v[None, :, None, :]
    sv = sin_v[None, :, None, :]
    cosines = (cu * cv - su * sv).reshape(TRANS, row_total, NF)
    sines = (su * cv + cu * sv).reshape(TRANS, row_total, NF)
    real_part = slice_rows[None, :, :NF]
    imag_part = slice_rows[None, :, NF:]
    shifted = jnp.concatenate([real_part * cosines - imag_part * sines, real_part * sines + imag_part * cosines], axis=-1).astype(jnp.bfloat16)
    flat_refs = shifted.reshape(TRANS, -1)
    return lax.dot_general(weighted, flat_refs, (((1,), (1,)), ((), ())), preferred_element_type=jnp.float32) / NF

def reference(pencils, send_map, interp_index, interp_frac, ori_count, spectra, class_ids, ctf_table):
    complex_lines = pencils[..., :NF] + 1j * pencils[..., NF:]
    spectrum = jnp.fft.fft(complex_lines, axis=2) / math.sqrt(NF)
    spectrum = jnp.transpose(spectrum, (2, 0, 1))
    volume_rows = jnp.concatenate([jnp.real(spectrum), jnp.imag(spectrum)], axis=-1).astype(jnp.bfloat16).reshape(NF * NF, 2 * NF)
    slab_starts = jnp.arange(N_SLAB, dtype=jnp.int32) * SLAB_ROWS
    row_group = jnp.arange(NF, dtype=jnp.int32) // (NF // N_GRP)
    factors = phase_factors(0, NF)

    def owner_scores(owner_id):
        slot_map = lax.dynamic_index_in_dim(send_map, owner_id, 2, keepdims=False)
        slot_map = jnp.transpose(slot_map, (1, 0, 2))
        global_rows = (slab_starts[None, :, None] + jnp.maximum(slot_map, 0)).reshape(-1)
        picked = jnp.take(volume_rows, global_rows, axis=0)
        picked = picked * (slot_map >= 0).reshape(-1, 1).astype(jnp.bfloat16)
        tap_index = lax.dynamic_index_in_dim(interp_index, owner_id, 1, keepdims=False)
        weights_tap = lax.dynamic_index_in_dim(interp_frac, owner_id, 0, keepdims=False)[..., None]
        lower_rows = jnp.take(picked, (row_group[None, :] * SLOTS + tap_index[0]).reshape(-1), axis=0).reshape(ORI_MAX, NF, 2 * NF)
        upper_rows = jnp.take(picked, (row_group[None, :] * SLOTS + tap_index[1]).reshape(-1), axis=0).reshape(ORI_MAX, NF, 2 * NF)
        slices = (1.0 - weights_tap) * lower_rows.astype(jnp.float32) + weights_tap * upper_rows.astype(jnp.float32)
        batch = lax.dynamic_slice_in_dim(spectra, owner_id * PART_DEV, PART_DEV, 0)
        classes = lax.dynamic_slice_in_dim(class_ids, owner_id * PART_DEV, PART_DEV, 0)
        ctf_rows = jnp.take(ctf_table, classes, axis=0).astype(jnp.float32)
        weighted = (jnp.concatenate([ctf_rows, ctf_rows], axis=-1) * batch.astype(jnp.float32)).astype(jnp.bfloat16).reshape(PART_DEV, -1)
        live_count = ori_count[owner_id]

        def orient_score(orient):
            result = shift_score(slices[orient], weighted, factors)
            return jnp.where(orient < live_count, result, jnp.zeros_like(result))
        blocks_out = lax.map(orient_score, jnp.arange(ORI_MAX, dtype=jnp.int32))
        return jnp.transpose(blocks_out, (1, 0, 2)).reshape(PART_DEV, ORI_MAX * TRANS)
    result = lax.map(owner_scores, jnp.arange(N_SLAB, dtype=jnp.int32))
    return result.reshape(PARTICLES, ORI_MAX * TRANS)
```

```python
import math

import jax
import jax.numpy as jnp
import ml_dtypes
import numpy as np
from jax import lax
from jax.experimental import pallas as pl
from jax.experimental.pallas import tpu as pltpu
from jax.sharding import PartitionSpec as P

NF = 256
CAP = 16
ORI_MAX = 8
TSIDE = 8
CLASSES = 16
PART_DEV = 8
TRANS = 64
N_GRP = 4
COLS = NF // N_GRP
LANES = 2 * COLS
SLAB_ROWS = 512
VMEM_BYTES = 48 * 1024 * 1024


def split_bf16(values):
    high = values.astype(ml_dtypes.bfloat16)
    low = (values - high.astype(np.float64)).astype(ml_dtypes.bfloat16)
    return high, low


def fourier_tables():
    index = np.arange(NF)
    angle = 2.0 * math.pi / NF * ((index[:, None] * index[None, :]) % NF)
    table = np.concatenate([np.cos(angle), np.sin(angle)], axis=1) / math.sqrt(NF)
    return np.stack(split_bf16(table))


def column_table():
    b = np.arange(TRANS) % TSIDE - TSIDE // 2
    v = np.arange(NF)
    angle = -2.0 * math.pi / NF * ((b[None, :] * v[:, None]) % NF)
    fr = np.cos(angle).reshape(N_GRP, COLS, TRANS) / NF
    fi = np.sin(angle).reshape(N_GRP, COLS, TRANS) / NF

    def lanes(first, second):
        return np.stack([first, second], axis=1).reshape(2 * NF, TRANS)

    with_er = np.concatenate([lanes(fr, fr), lanes(-fi, fi)], axis=0)
    with_ei = np.concatenate([lanes(-fi, -fi), lanes(-fr, fr)], axis=0)
    high, low = split_bf16(np.concatenate([with_er, with_ei], axis=1))
    return np.concatenate([high, low], axis=1)


def row_table():
    a = np.arange(TRANS) // TSIDE - TSIDE // 2
    u = np.arange(NF)
    angle = -2.0 * math.pi / NF * ((a[None, :] * u[:, None]) % NF)
    table = np.concatenate([np.cos(angle), np.sin(angle)], axis=1).astype(np.float32)
    return table.reshape(N_GRP, COLS, 2 * TRANS)


def fourier_kernel(x_ref, table_ref, out_ref, wide):
    contract = (((1,), (1,)), ((), ()))
    for ky in range(2):
        lines = x_ref[ky]
        turned = jnp.concatenate([lines[:, NF:], -lines[:, :NF]], axis=1)
        both = jnp.concatenate([lines, turned], axis=0)
        high = both.astype(jnp.bfloat16)
        low = (both - high.astype(jnp.float32)).astype(jnp.bfloat16)

        def product(table, part):
            return lax.dot_general(table, part, contract, preferred_element_type=jnp.float32)

        result = (product(table_ref[0], low) + product(table_ref[1], high)) + product(
            table_ref[0], high
        )
        wide[pl.ds(ky, NF, stride=2), :] = result
    out_ref[...] = wide[...].astype(jnp.bfloat16)


def fourier(pencils, table):
    return pl.pallas_call(
        fourier_kernel,
        out_shape=jax.ShapeDtypeStruct((2 * NF, LANES), jnp.bfloat16),
        scratch_shapes=[pltpu.VMEM((2 * NF, LANES), jnp.float32)],
        compiler_params=pltpu.CompilerParams(vmem_limit_bytes=VMEM_BYTES),
        cost_estimate=pl.CostEstimate(
            flops=6 * NF * NF * 2 * NF, bytes_accessed=1 << 20, transcendentals=0
        ),
    )(pencils, table)


PICK_STEP = 512


def pick_kernel(place_ref, table_ref, out_ref):
    place = place_ref[...]
    lane = lax.broadcasted_iota(jnp.int32, (PICK_STEP, LANES), 1)
    hits = jnp.concatenate(
        [
            jnp.where(place == lane + first, 1.0, 0.0).astype(jnp.bfloat16)
            for first in range(0, SLAB_ROWS, LANES)
        ],
        axis=1,
    )
    rows = jnp.concatenate([table_ref[g] for g in range(N_GRP)], axis=1)
    out_ref[...] = jnp.dot(hits, rows, preferred_element_type=jnp.float32).astype(jnp.bfloat16)


def pick(place, table):
    total = place.shape[0]
    return pl.pallas_call(
        pick_kernel,
        grid=(total // PICK_STEP,),
        in_specs=[
            pl.BlockSpec((PICK_STEP, LANES), lambda i: (i, 0)),
            pl.BlockSpec((N_GRP, SLAB_ROWS, LANES), lambda i: (0, 0, 0)),
        ],
        out_specs=pl.BlockSpec((PICK_STEP, 2 * NF), lambda i: (i, 0)),
        out_shape=jax.ShapeDtypeStruct((total, 2 * NF), jnp.bfloat16),
        compiler_params=pltpu.CompilerParams(vmem_limit_bytes=VMEM_BYTES),
        cost_estimate=pl.CostEstimate(
            flops=2 * total * SLAB_ROWS * 2 * NF, bytes_accessed=4 << 20, transcendentals=0
        ),
    )(place, table)


def score_kernel(
    count_ref, buffer_ref, tap_ref, frac_ref, weighted_ref, col_ref, row_ref, out_ref, mix, slices
):
    total = tap_ref.shape[1]
    slots = buffer_ref.shape[0]
    lane = lax.broadcasted_iota(jnp.int32, (total, LANES), 1)
    frac = frac_ref[...]
    rest = 1.0 - frac
    for first in range(0, slots, LANES):
        entry = jnp.where(tap_ref[0] == lane + first, rest, 0.0) + jnp.where(
            tap_ref[1] == lane + first, frac, 0.0
        )
        high = entry.astype(jnp.bfloat16)
        low = (entry - high.astype(jnp.float32)).astype(jnp.bfloat16)
        mix[:total, first : first + LANES] = high
        mix[total:, first : first + LANES] = low
    both = jnp.dot(mix[...], buffer_ref[...], preferred_element_type=jnp.float32)
    slices[...] = both[:total] + both[total:]
    live_count = count_ref[0]
    phase_rows = row_ref[...]
    left = lax.broadcasted_iota(jnp.int32, (PART_DEV, LANES), 1) < TRANS
    for pair in range(ORI_MAX // 2):
        done = []
        for orient in (2 * pair, 2 * pair + 1):
            plain = slices[orient * COLS : (orient + 1) * COLS, :]
            swapped = jnp.concatenate(
                [
                    pltpu.roll(plain[:, first : first + LANES], COLS, 1)
                    for first in range(0, 2 * NF, LANES)
                ],
                axis=1,
            )
            shifted = jnp.concatenate([plain, swapped], axis=1)
            products = []
            for particle in range(PART_DEV):
                weight = weighted_ref[particle].astype(jnp.float32)
                products.append(
                    (jnp.concatenate([weight, weight], axis=1) * shifted).astype(jnp.bfloat16)
                )
            columns = jnp.dot(
                jnp.concatenate(products, axis=0),
                col_ref[...],
                preferred_element_type=jnp.float32,
            )
            columns = columns[:, :LANES] + columns[:, LANES:]
            summed = jnp.sum(columns.reshape(PART_DEV, COLS, LANES) * phase_rows[None], axis=1)
            folded = summed + pltpu.roll(summed, TRANS, 1)
            done.append(jnp.where(orient < live_count, folded, 0.0))
        out_ref[pair] = jnp.where(left, done[0], done[1])


def score(count, buffer, taps, frac, weighted, col_phase, row_phase):
    total = taps.shape[1]
    vmem = pl.BlockSpec(memory_space=pltpu.VMEM)
    return pl.pallas_call(
        score_kernel,
        in_specs=[pl.BlockSpec(memory_space=pltpu.SMEM)] + [vmem] * 6,
        out_specs=vmem,
        out_shape=jax.ShapeDtypeStruct((ORI_MAX // 2, PART_DEV, 2 * TRANS), jnp.float32),
        scratch_shapes=[
            pltpu.VMEM((2 * total, buffer.shape[0]), jnp.bfloat16),
            pltpu.VMEM((total, 2 * NF), jnp.float32),
        ],
        compiler_params=pltpu.CompilerParams(vmem_limit_bytes=VMEM_BYTES),
        cost_estimate=pl.CostEstimate(
            flops=4 << 30, bytes_accessed=4 << 20, transcendentals=0
        ),
    )(count, buffer, taps, frac, weighted, col_phase, row_phase)


def shards(pencils, send_map, interp_index, interp_frac, ori_count, spectra, class_ids, ctf_table):
    planes = fourier(pencils, jnp.asarray(fourier_tables()))
    slab_planes = lax.all_to_all(planes, "slab", split_axis=0, concat_axis=0, tiled=True)
    table = lax.all_gather(slab_planes, "grp", axis=0)
    wanted = jnp.maximum(send_map[0, 0], 0)
    place = ((wanted & (NF - 2)) << 1) | ((wanted >> 8) << 1) | (wanted & 1)
    outgoing = pick(jnp.broadcast_to(place.reshape(-1, 1), (place.size, LANES)), table)
    buffer = lax.all_to_all(outgoing, "slab", split_axis=0, concat_axis=0, tiled=True)

    rows_local = interp_frac.shape[2]
    total = ORI_MAX * rows_local
    taps = jnp.broadcast_to(interp_index.reshape(2, total, 1), (2, total, LANES))
    frac = jnp.broadcast_to(interp_frac.reshape(total, 1), (total, LANES))
    onehot = (class_ids[:, None] == jnp.arange(CLASSES, dtype=jnp.int32)[None, :]).astype(
        jnp.bfloat16
    )
    ctf_rows = jnp.dot(
        onehot, ctf_table.reshape(CLASSES, -1), preferred_element_type=jnp.float32
    ).reshape(PART_DEV, rows_local, N_GRP, 1, COLS)
    by_group = spectra.reshape(PART_DEV, rows_local, 2, N_GRP, COLS).transpose(0, 1, 3, 2, 4)
    weighted = (
        (ctf_rows * by_group.astype(jnp.float32))
        .astype(jnp.bfloat16)
        .reshape(PART_DEV, rows_local, 2 * NF)
    )
    row_phase = lax.dynamic_index_in_dim(
        jnp.asarray(row_table()), lax.axis_index("grp"), 0, keepdims=False
    )
    partial = score(
        ori_count, buffer, taps, frac, weighted, jnp.asarray(column_table()), row_phase
    )
    parts = lax.all_to_all(partial, "grp", split_axis=0, concat_axis=0, tiled=True)
    return jnp.sum(parts, axis=0)


def solution(mesh):
    return jax.shard_map(
        shards,
        mesh=mesh,
        in_specs=(
            P("slab", "grp", None),
            P("slab", "grp", None, None),
            P(None, "slab", None, "grp"),
            P("slab", None, "grp"),
            P("slab"),
            P("slab", "grp", None),
            P("slab"),
            P(None, "grp", None),
        ),
        out_specs=P("slab", "grp"),
        check_vma=False,
    )
```

```python
import math

import jax
import jax.numpy as jnp
import ml_dtypes
import numpy as np
from jax import lax
from jax.experimental import pallas as pl
from jax.experimental.pallas import tpu as pltpu
from jax.sharding import Mesh
from jax.sharding import PartitionSpec as P

NF = 256
CAP = 16
ORI_MAX = 8
TSIDE = 8
PART_DEV = 8
TRANS = 64
N_GRP = 4
COLS = NF // N_GRP
LANES = 2 * COLS
SLAB_ROWS = 512
SLOTS = 2048
TAKES = ORI_MAX * COLS
PARTICLE_ROWS = PART_DEV * COLS
EXTRA_ROWS = 32
VMEM_BYTES = 48 * 1024 * 1024
SLAB_AXES = ("y", "h", "l", "c")
ROW_AXES = ("x", "y", "l", "c")


def split_bf16(values):
    high = values.astype(ml_dtypes.bfloat16)
    low = (values - high.astype(np.float64)).astype(ml_dtypes.bfloat16)
    return high, low


def fourier_tables():
    index = np.arange(NF)
    angle = 2.0 * math.pi / NF * ((index[:, None] * index[None, :]) % NF)
    table = np.concatenate([np.cos(angle), np.sin(angle)], axis=1) / math.sqrt(NF)
    return np.stack(split_bf16(table))


def column_table():
    b = np.arange(TRANS) % TSIDE - TSIDE // 2
    v = np.arange(NF)
    angle = -2.0 * math.pi / NF * ((b[None, :] * v[:, None]) % NF)
    fr = np.cos(angle).reshape(N_GRP, COLS, TRANS) / NF
    fi = np.sin(angle).reshape(N_GRP, COLS, TRANS) / NF
    with_er = np.concatenate([fr, fr, -fi, fi], axis=1)
    with_ei = np.concatenate([-fi, -fi, -fr, fr], axis=1)
    high, low = split_bf16(np.concatenate([with_er, with_ei], axis=2))
    return np.concatenate([high, low], axis=2)


def row_table():
    a = np.arange(TRANS) // TSIDE - TSIDE // 2
    u = np.arange(NF)
    angle = -2.0 * math.pi / NF * ((a[None, :] * u[:, None]) % NF)
    table = np.concatenate([np.cos(angle), np.sin(angle)], axis=1).astype(np.float32)
    return table.reshape(N_GRP, COLS, 2 * TRANS)


def down_rows(row):
    return jnp.broadcast_to(row, (LANES, LANES)).T


def fourier_kernel(x_ref, table_ref, out_ref, wide):
    contract = (((1,), (1,)), ((), ()))
    for ky in range(2):
        lines = x_ref[ky]
        turned = jnp.concatenate([lines[:, NF:], -lines[:, :NF]], axis=1)
        both = jnp.concatenate([lines, turned], axis=0)
        high = both.astype(jnp.bfloat16)
        low = (both - high.astype(jnp.float32)).astype(jnp.bfloat16)

        def product(table, part):
            return lax.dot_general(table, part, contract, preferred_element_type=jnp.float32)

        result = (product(table_ref[0], low) + product(table_ref[1], high)) + product(
            table_ref[0], high
        )
        wide[pl.ds(ky, NF, stride=2), :] = result
    rest = 32
    for y in range(4):
        for h in range(4):
            out_ref[(h * 4 + y) * rest : (h * 4 + y + 1) * rest, :] = wide[
                (y * 4 + h) * rest : (y * 4 + h + 1) * rest, :
            ].astype(jnp.bfloat16)


def fourier(pencils, table):
    return pl.pallas_call(
        fourier_kernel,
        out_shape=jax.ShapeDtypeStruct((2 * NF, LANES), jnp.bfloat16),
        scratch_shapes=[pltpu.VMEM((2 * NF, LANES), jnp.float32)],
        compiler_params=pltpu.CompilerParams(vmem_limit_bytes=VMEM_BYTES),
        cost_estimate=pl.CostEstimate(
            flops=6 * NF * NF * 2 * NF, bytes_accessed=1 << 20, transcendentals=0
        ),
    )(pencils, table)


def weigh_kernel(class_ref, spectra_ref, ctf_ref, taps_ref, out_ref):
    for particle in range(PART_DEV):
        factor = ctf_ref[class_ref[particle]].astype(jnp.float32)
        lines = spectra_ref[particle].astype(jnp.float32)
        real = lines[:, :NF] * factor
        imag = lines[:, NF:] * factor
        for part in range(N_GRP):
            span = slice(part * COLS, (part + 1) * COLS)
            out_ref[part, particle * COLS : (particle + 1) * COLS, :] = jnp.concatenate(
                [real[:, span], imag[:, span]], axis=1
            ).astype(jnp.bfloat16)
    taps = taps_ref[...]
    place = taps[:8]
    place_high = jnp.floor(place * (1.0 / 16.0))
    place_low = place - 16.0 * place_high
    frac = taps[8:12]
    first = frac.astype(jnp.bfloat16).astype(jnp.float32)
    second = (frac - first).astype(jnp.bfloat16).astype(jnp.float32)
    third = frac - first - second
    extra = jnp.concatenate(
        [place_high, place_low, first, second, third, jnp.zeros_like(frac)], axis=0
    ).astype(jnp.bfloat16)
    for part in range(N_GRP):
        out_ref[part, PARTICLE_ROWS:, :] = extra


def weigh(class_ids, spectra, ctf_table, taps):
    vmem = pl.BlockSpec(memory_space=pltpu.VMEM)
    return pl.pallas_call(
        weigh_kernel,
        in_specs=[pl.BlockSpec(memory_space=pltpu.SMEM)] + [vmem] * 3,
        out_specs=vmem,
        out_shape=jax.ShapeDtypeStruct((N_GRP, PARTICLE_ROWS + EXTRA_ROWS, LANES), jnp.bfloat16),
        compiler_params=pltpu.CompilerParams(vmem_limit_bytes=VMEM_BYTES),
        cost_estimate=pl.CostEstimate(flops=1 << 20, bytes_accessed=2 << 20, transcendentals=0),
    )(class_ids, spectra, ctf_table, taps)


PICK_STEP = 1024


def pick_kernel(order_ref, place_ref, table_ref, out_ref):
    del order_ref
    lane = lax.broadcasted_iota(jnp.int32, (LANES, LANES), 1).astype(jnp.float32)
    blocks = []
    for row in range(PICK_STEP // LANES):
        place = down_rows(place_ref[row : row + 1, :])
        blocks.append(
            jnp.concatenate(
                [
                    jnp.where(place == lane + float(first), 1.0, 0.0).astype(jnp.bfloat16)
                    for first in range(0, SLAB_ROWS, LANES)
                ],
                axis=1,
            )
        )
    hits = jnp.concatenate(blocks, axis=0)
    out_ref[...] = jnp.dot(hits, table_ref[...], preferred_element_type=jnp.float32).astype(
        jnp.bfloat16
    )


def pick(order, place, table):
    total = place.size
    halves = total // N_GRP // PICK_STEP
    return pl.pallas_call(
        pick_kernel,
        grid_spec=pltpu.PrefetchScalarGridSpec(
            num_scalar_prefetch=1,
            grid=(N_GRP, halves),
            in_specs=[
                pl.BlockSpec(
                    (PICK_STEP // LANES, LANES), lambda g, i, order: (order[g] * halves + i, 0)
                ),
                pl.BlockSpec((SLAB_ROWS, LANES), lambda g, i, order: (0, 0)),
            ],
            out_specs=pl.BlockSpec((PICK_STEP, LANES), lambda g, i, order: (g * halves + i, 0)),
        ),
        out_shape=jax.ShapeDtypeStruct((total, LANES), jnp.bfloat16),
        compiler_params=pltpu.CompilerParams(vmem_limit_bytes=VMEM_BYTES),
        cost_estimate=pl.CostEstimate(
            flops=2 * total * SLAB_ROWS * LANES, bytes_accessed=4 << 20, transcendentals=0
        ),
    )(order, place, table)


def score_kernel(order_ref, buffer_ref, weighted_ref, col_ref, row_ref, out_ref, mix, slices):
    del order_ref
    lane = lax.broadcasted_iota(jnp.int32, (LANES, LANES), 1).astype(jnp.float32)
    extra = weighted_ref[PARTICLE_ROWS:, :].astype(jnp.float32)
    place = 16.0 * extra[:8] + extra[8:16]
    frac = extra[16:20] + extra[20:24] + extra[24:28]
    for row in range(8):
        column = down_rows(place[row : row + 1])
        for first in range(0, SLOTS, LANES):
            mix[row * LANES : (row + 1) * LANES, first : first + LANES] = jnp.where(
                column == lane + float(first), 1.0, 0.0
            ).astype(jnp.bfloat16)
    taken = jnp.dot(
        mix[...], buffer_ref[...].reshape(SLOTS, LANES), preferred_element_type=jnp.float32
    )
    for row in range(4):
        share = down_rows(frac[row : row + 1])
        span = slice(row * LANES, (row + 1) * LANES)
        slices[span, :] = (1.0 - share) * taken[span] + share * taken[TAKES:][span]
    phase_rows = row_ref[...]
    left = lax.broadcasted_iota(jnp.int32, (PART_DEV, LANES), 1) < TRANS
    weight = weighted_ref[:PARTICLE_ROWS, :].astype(jnp.float32).reshape(PART_DEV, COLS, LANES)
    for pair in range(ORI_MAX // 2):
        done = []
        for orient in (2 * pair, 2 * pair + 1):
            plain = slices[orient * COLS : (orient + 1) * COLS, :]
            swapped = pltpu.roll(plain, COLS, 1)
            products = jnp.concatenate(
                [
                    (weight * plain[None]).astype(jnp.bfloat16),
                    (weight * swapped[None]).astype(jnp.bfloat16),
                ],
                axis=-1,
            ).reshape(PARTICLE_ROWS, 2 * LANES)
            columns = jnp.dot(products, col_ref[...], preferred_element_type=jnp.float32)
            columns = columns[:, :LANES] + columns[:, LANES:]
            summed = jnp.sum(columns.reshape(PART_DEV, COLS, LANES) * phase_rows[None], axis=1)
            done.append(summed + pltpu.roll(summed, TRANS, 1))
        out_ref[pair] = jnp.where(left, done[0], done[1])


def score(order, buffer, weighted, col_phase, row_phase):
    return pl.pallas_call(
        score_kernel,
        grid_spec=pltpu.PrefetchScalarGridSpec(
            num_scalar_prefetch=1,
            grid=(N_GRP,),
            in_specs=[
                pl.BlockSpec(
                    (SLOTS // CAP, None, CAP, LANES), lambda i, order: (0, order[i], 0, 0)
                ),
                pl.BlockSpec(
                    (None, PARTICLE_ROWS + EXTRA_ROWS, LANES), lambda i, order: (i, 0, 0)
                ),
                pl.BlockSpec((2 * LANES, 2 * LANES), lambda i, order: (0, 0)),
                pl.BlockSpec((COLS, LANES), lambda i, order: (0, 0)),
            ],
            out_specs=pl.BlockSpec(
                (None, ORI_MAX // 2, PART_DEV, LANES), lambda i, order: (order[i], 0, 0, 0)
            ),
            scratch_shapes=[
                pltpu.VMEM((2 * TAKES, SLOTS), jnp.bfloat16),
                pltpu.VMEM((TAKES, LANES), jnp.float32),
            ],
        ),
        out_shape=jax.ShapeDtypeStruct((N_GRP, ORI_MAX // 2, PART_DEV, LANES), jnp.float32),
        compiler_params=pltpu.CompilerParams(vmem_limit_bytes=VMEM_BYTES),
        cost_estimate=pl.CostEstimate(flops=8 << 30, bytes_accessed=4 << 20, transcendentals=0),
    )(order, buffer, weighted, col_phase, row_phase)


def exchange(values, axes):
    return lax.all_to_all(values, axes, split_axis=0, concat_axis=0, tiled=True)


def own_part(table, axis):
    return lax.dynamic_index_in_dim(jnp.asarray(table), lax.axis_index(axis), 0, keepdims=False)


def shards(pencils, send_map, interp_index, interp_frac, ori_count, spectra, class_ids, ctf_table):
    here = lax.axis_index("h")
    turn = jnp.arange(4, dtype=jnp.int32)
    planes = exchange(fourier(pencils, jnp.asarray(fourier_tables())), "x")
    planes = planes.reshape(4, 4, 32, LANES).transpose(1, 0, 2, 3).reshape(2 * NF, LANES)

    wanted, planes = lax.optimization_barrier((send_map[0, 0], planes))
    table = exchange(planes, SLAB_AXES)
    wanted = jnp.maximum(wanted, 0)
    place = ((wanted & (NF - 2)) << 1) | ((wanted >> 8) << 1) | (wanted & 1)
    place = place.reshape(4, 4, 8, CAP).transpose(0, 2, 1, 3).reshape(CAP, LANES)
    place = place.astype(jnp.float32)
    maps = [
        lax.ppermute(
            place,
            ("h", "x"),
            [(slab * 4 + g, (g + j) % 4 * 4 + slab) for g in range(4) for slab in range(4)],
        )
        for j in range(4)
    ]
    outgoing = pick((here - turn) % 4, jnp.concatenate(maps, axis=0), table)

    slot = interp_index.reshape(2, TAKES)
    source = slot >> 4
    source = (((source >> 3) & 3) << 5) | ((source >> 5) << 3) | (source & 7)
    slot = ((source << 4) | (slot & 15)).astype(jnp.float32)
    taps = jnp.concatenate([slot.reshape(8, LANES), interp_frac.reshape(4, LANES)], axis=0)
    weighted, outgoing = lax.optimization_barrier(
        (weigh(class_ids, spectra, ctf_table, taps), outgoing)
    )
    buffer = exchange(outgoing, ROW_AXES).reshape(SLOTS // CAP, 4, CAP, LANES)
    owners = [lax.dynamic_index_in_dim(weighted, here, 0, keepdims=False)]
    for k in range(1, 4):
        block = lax.dynamic_index_in_dim(weighted, (here - k) % 4, 0, keepdims=False)
        owners.append(lax.ppermute(block, "h", [((i + k) % 4, i) for i in range(4)]))
    partial = score(
        (here + turn) % 4,
        buffer,
        jnp.stack(owners),
        own_part(column_table(), "h"),
        own_part(row_table(), "x"),
    )
    parts = exchange(partial.reshape(16, PART_DEV, LANES), ("h", "x"))
    total = jnp.sum(parts, axis=0)
    orient = 2 * lax.axis_index("x") + jnp.arange(LANES, dtype=jnp.int32) // TRANS
    return jnp.where(orient[None, :] < ori_count[0], total, 0.0)


def solution(mesh):
    fine = Mesh(mesh.devices.reshape(4, 4, 4, 2, 4), SLAB_AXES + ("x",))
    return jax.shard_map(
        shards,
        mesh=fine,
        in_specs=(
            P(SLAB_AXES, "x", None),
            P(SLAB_AXES, "x", None, None),
            P(None, SLAB_AXES, None, "x"),
            P(SLAB_AXES, None, "x"),
            P(SLAB_AXES),
            P(SLAB_AXES, "x", None),
            P(SLAB_AXES),
            P(None, "x", None),
        ),
        out_specs=P(SLAB_AXES, "x"),
        check_vma=False,
    )
```

```python
import math

import jax
import jax.numpy as jnp
import ml_dtypes
import numpy as np
from jax import lax
from jax.experimental import pallas as pl
from jax.experimental.pallas import tpu as pltpu
from jax.sharding import Mesh
from jax.sharding import PartitionSpec as P

NF = 256
CAP = 16
ORI_MAX = 8
TSIDE = 8
PART_DEV = 8
TRANS = 64
N_GRP = 4
COLS = NF // N_GRP
LANES = 2 * COLS
SLAB_ROWS = 512
SLOTS = 2048
TAKES = ORI_MAX * COLS
PARTICLE_ROWS = PART_DEV * COLS
EXTRA_ROWS = 32
VMEM_BYTES = 48 * 1024 * 1024
SLAB_AXES = ("y", "h", "l", "c")
ROW_AXES = ("y", "l", "c")


def split_bf16(values):
    high = values.astype(ml_dtypes.bfloat16)
    low = (values - high.astype(np.float64)).astype(ml_dtypes.bfloat16)
    return high, low


def fourier_tables():
    index = np.arange(NF)
    kz = index.reshape(4, 4, 8, 2).transpose(0, 2, 3, 1).reshape(NF)
    angle = 2.0 * math.pi / NF * ((kz[:, None] * index[None, :]) % NF)
    table = np.concatenate([np.cos(angle), np.sin(angle)], axis=1) / math.sqrt(NF)
    return np.stack(split_bf16(table))


def column_table():
    b = np.arange(TRANS) % TSIDE - TSIDE // 2
    v = np.arange(NF)
    angle = -2.0 * math.pi / NF * ((b[None, :] * v[:, None]) % NF)
    fr = np.cos(angle).reshape(N_GRP, COLS, TRANS) / NF
    fi = np.sin(angle).reshape(N_GRP, COLS, TRANS) / NF
    with_er = np.concatenate([fr, fr, -fi, fi], axis=1)
    with_ei = np.concatenate([-fi, -fi, -fr, fr], axis=1)
    high, low = split_bf16(np.concatenate([with_er, with_ei], axis=2))
    return np.concatenate([high, low], axis=2)


def row_table():
    a = np.arange(TRANS) // TSIDE - TSIDE // 2
    u = np.arange(NF)
    angle = -2.0 * math.pi / NF * ((a[None, :] * u[:, None]) % NF)
    table = np.concatenate([np.cos(angle), np.sin(angle)], axis=1).astype(np.float32)
    return table.reshape(N_GRP, COLS, 2 * TRANS)


def down_rows(row):
    return jnp.broadcast_to(row, (LANES, LANES)).T


def hit_tiles(row, total):
    high = jnp.floor(row * (1.0 / LANES))
    low = down_rows(row - float(LANES) * high).astype(jnp.bfloat16)
    high = down_rows(high).astype(jnp.bfloat16)
    lane = lax.broadcasted_iota(jnp.int32, (LANES, LANES), 1).astype(jnp.float32)
    inner = jnp.where(low == lane.astype(jnp.bfloat16), 1.0, 0.0).astype(jnp.bfloat16)
    zero = jnp.zeros_like(inner)
    return [
        jnp.where(high == jnp.full_like(high, float(tile)), inner, zero)
        for tile in range(total // LANES)
    ]


def fourier_kernel(x_ref, table_ref, out_ref, wide):
    contract = (((1,), (1,)), ((), ()))
    for ky in range(2):
        lines = x_ref[ky]
        turned = jnp.concatenate([lines[:, NF:], -lines[:, :NF]], axis=1)
        both = jnp.concatenate([lines, turned], axis=0)
        high = both.astype(jnp.bfloat16)
        low = (both - high.astype(jnp.float32)).astype(jnp.bfloat16)

        def product(table, part):
            return lax.dot_general(table, part, contract, preferred_element_type=jnp.float32)

        result = (product(table_ref[0], low) + product(table_ref[1], high)) + product(
            table_ref[0], high
        )
        wide[pl.ds(ky, NF, stride=2), :] = result
    rest = 2 * NF // 4
    for y in range(4):
        block = wide[y * rest : (y + 1) * rest, :].astype(jnp.bfloat16)
        for h in range(4):
            out_ref[(y * 4 + h) * rest : (y * 4 + h + 1) * rest, :] = block


def fourier(pencils, table):
    return pl.pallas_call(
        fourier_kernel,
        out_shape=jax.ShapeDtypeStruct((8 * NF, LANES), jnp.bfloat16),
        scratch_shapes=[pltpu.VMEM((2 * NF, LANES), jnp.float32)],
        compiler_params=pltpu.CompilerParams(vmem_limit_bytes=VMEM_BYTES),
        cost_estimate=pl.CostEstimate(
            flops=6 * NF * NF * 2 * NF, bytes_accessed=1 << 20, transcendentals=0
        ),
    )(pencils, table)


def weigh_kernel(class_ref, spectra_ref, ctf_ref, taps_ref, out_ref):
    for particle in range(PART_DEV):
        factor = ctf_ref[class_ref[particle]].astype(jnp.float32)
        lines = spectra_ref[particle].astype(jnp.float32)
        real = lines[:, :NF] * factor
        imag = lines[:, NF:] * factor
        for part in range(N_GRP):
            span = slice(part * COLS, (part + 1) * COLS)
            out_ref[part, particle * COLS : (particle + 1) * COLS, :] = jnp.concatenate(
                [real[:, span], imag[:, span]], axis=1
            ).astype(jnp.bfloat16)
    taps = taps_ref[...]
    place = taps[:8]
    place_high = jnp.floor(place * (1.0 / 16.0))
    place_low = place - 16.0 * place_high
    frac = taps[8:12]
    first = frac.astype(jnp.bfloat16).astype(jnp.float32)
    second = (frac - first).astype(jnp.bfloat16).astype(jnp.float32)
    third = frac - first - second
    extra = jnp.concatenate(
        [place_high, place_low, first, second, third, jnp.zeros_like(frac)], axis=0
    ).astype(jnp.bfloat16)
    for part in range(N_GRP):
        out_ref[part, PARTICLE_ROWS:, :] = extra


def weigh(class_ids, spectra, ctf_table, taps):
    vmem = pl.BlockSpec(memory_space=pltpu.VMEM)
    return pl.pallas_call(
        weigh_kernel,
        in_specs=[pl.BlockSpec(memory_space=pltpu.SMEM)] + [vmem] * 3,
        out_specs=vmem,
        out_shape=jax.ShapeDtypeStruct((N_GRP, PARTICLE_ROWS + EXTRA_ROWS, LANES), jnp.bfloat16),
        compiler_params=pltpu.CompilerParams(vmem_limit_bytes=VMEM_BYTES),
        cost_estimate=pl.CostEstimate(flops=1 << 20, bytes_accessed=2 << 20, transcendentals=0),
    )(class_ids, spectra, ctf_table, taps)


def pick_kernel(place_ref, table_ref, out_ref, wide, slabs, hits):
    @pl.when(pl.program_id(0) == 0)
    def _():
        wide[...] = table_ref[...].astype(jnp.float32)
        for slab in range(4):
            for ky in range(2):
                slabs[slab, ky * NF : (ky + 1) * NF, :] = wide[
                    pl.ds(2 * slab + ky, NF, stride=8), :
                ].astype(jnp.bfloat16)

    for slab in range(4):
        for row in range(4):
            tiles = hit_tiles(place_ref[slab * 4 + row : slab * 4 + row + 1, :], SLAB_ROWS)
            for at, tile in enumerate(tiles):
                hits[row * LANES : (row + 1) * LANES, at * LANES : (at + 1) * LANES] = tile
        taken = jnp.dot(hits[...], slabs[slab], preferred_element_type=jnp.float32)
        out_ref[:, slab, :, :] = taken.astype(jnp.bfloat16).reshape(32, CAP, LANES)


def pick(place, table):
    return pl.pallas_call(
        pick_kernel,
        grid=(N_GRP,),
        in_specs=[
            pl.BlockSpec((CAP, LANES), lambda g: (g, 0)),
            pl.BlockSpec((4 * SLAB_ROWS, LANES), lambda g: (0, 0)),
        ],
        out_specs=pl.BlockSpec((32, None, 4, CAP, LANES), lambda g: (0, g, 0, 0, 0)),
        out_shape=jax.ShapeDtypeStruct((32, N_GRP, 4, CAP, LANES), jnp.bfloat16),
        scratch_shapes=[
            pltpu.VMEM((4 * SLAB_ROWS, LANES), jnp.float32),
            pltpu.VMEM((4, SLAB_ROWS, LANES), jnp.bfloat16),
            pltpu.VMEM((SLAB_ROWS, SLAB_ROWS), jnp.bfloat16),
        ],
        compiler_params=pltpu.CompilerParams(vmem_limit_bytes=VMEM_BYTES),
        cost_estimate=pl.CostEstimate(
            flops=16 * SLOTS * SLAB_ROWS * LANES, bytes_accessed=4 << 20, transcendentals=0
        ),
    )(place, table)


def score_kernel(order_ref, buffer_ref, weighted_ref, col_ref, row_ref, out_ref, mix, slices):
    del order_ref
    extra = weighted_ref[PARTICLE_ROWS:, :].astype(jnp.float32)
    place = 16.0 * extra[:8] + extra[8:16]
    frac = extra[16:20] + extra[20:24] + extra[24:28]
    for row in range(8):
        for at, tile in enumerate(hit_tiles(place[row : row + 1], SLOTS)):
            mix[row * LANES : (row + 1) * LANES, at * LANES : (at + 1) * LANES] = tile
    taken = jnp.dot(
        mix[...], buffer_ref[...].reshape(SLOTS, LANES), preferred_element_type=jnp.float32
    )
    for row in range(4):
        share = down_rows(frac[row : row + 1])
        span = slice(row * LANES, (row + 1) * LANES)
        slices[span, :] = (1.0 - share) * taken[span] + share * taken[TAKES:][span]
    phase_rows = row_ref[...]
    left = lax.broadcasted_iota(jnp.int32, (PART_DEV, LANES), 1) < TRANS
    weight = weighted_ref[:PARTICLE_ROWS, :].astype(jnp.float32).reshape(PART_DEV, COLS, LANES)
    for pair in range(ORI_MAX // 2):
        done = []
        for orient in (2 * pair, 2 * pair + 1):
            plain = slices[orient * COLS : (orient + 1) * COLS, :]
            swapped = pltpu.roll(plain, COLS, 1)
            products = jnp.concatenate(
                [
                    (weight * plain[None]).astype(jnp.bfloat16),
                    (weight * swapped[None]).astype(jnp.bfloat16),
                ],
                axis=-1,
            ).reshape(PARTICLE_ROWS, 2 * LANES)
            columns = jnp.dot(products, col_ref[...], preferred_element_type=jnp.float32)
            columns = columns[:, :LANES] + columns[:, LANES:]
            summed = jnp.sum(columns.reshape(PART_DEV, COLS, LANES) * phase_rows[None], axis=1)
            done.append(summed + pltpu.roll(summed, TRANS, 1))
        total = jnp.where(left, done[0], done[1])

        @pl.when(pl.program_id(0) == 0)
        def _():
            out_ref[pair] = total

        @pl.when(pl.program_id(0) > 0)
        def _():
            out_ref[pair] += total


def score(order, buffer, weighted, col_phase, row_phase):
    return pl.pallas_call(
        score_kernel,
        grid_spec=pltpu.PrefetchScalarGridSpec(
            num_scalar_prefetch=1,
            grid=(N_GRP,),
            in_specs=[
                pl.BlockSpec(
                    (32, None, 4 * CAP, LANES), lambda i, order: (0, order[i], 0, 0)
                ),
                pl.BlockSpec(
                    (None, PARTICLE_ROWS + EXTRA_ROWS, LANES), lambda i, order: (i, 0, 0)
                ),
                pl.BlockSpec((2 * LANES, 2 * LANES), lambda i, order: (0, 0)),
                pl.BlockSpec((None, COLS, LANES), lambda i, order: (order[i], 0, 0)),
            ],
            out_specs=pl.BlockSpec(
                (ORI_MAX // 2, PART_DEV, LANES), lambda i, order: (0, 0, 0)
            ),
            scratch_shapes=[
                pltpu.VMEM((2 * TAKES, SLOTS), jnp.bfloat16),
                pltpu.VMEM((TAKES, LANES), jnp.float32),
            ],
        ),
        out_shape=jax.ShapeDtypeStruct((ORI_MAX // 2, PART_DEV, LANES), jnp.float32),
        compiler_params=pltpu.CompilerParams(vmem_limit_bytes=VMEM_BYTES),
        cost_estimate=pl.CostEstimate(flops=8 << 30, bytes_accessed=4 << 20, transcendentals=0),
    )(order, buffer, weighted, col_phase, row_phase)


def exchange(values, axes):
    return lax.all_to_all(values, axes, split_axis=0, concat_axis=0, tiled=True)


def own_part(table, axis):
    return lax.dynamic_index_in_dim(jnp.asarray(table), lax.axis_index(axis), 0, keepdims=False)


def shards(pencils, send_map, interp_index, interp_frac, ori_count, spectra, class_ids, ctf_table):
    here = lax.axis_index("x")
    turn = jnp.arange(4, dtype=jnp.int32)
    table = exchange(fourier(pencils, jnp.asarray(fourier_tables())), SLAB_AXES)

    wanted = jnp.maximum(send_map[0, 0], 0)
    place = ((wanted & 1) << 8) | (wanted & (NF - 2)) | (wanted >> 8)
    place = place.astype(jnp.float32).reshape(4, 4, 8, CAP).transpose(1, 0, 2, 3)
    maps = lax.all_gather(place.reshape(4, 4, LANES), "h", axis=0)
    maps = lax.dynamic_index_in_dim(maps, lax.axis_index("h"), 1, keepdims=False)
    maps = lax.all_gather(maps.reshape(CAP, LANES), "x", axis=0, tiled=True)
    outgoing = pick(maps, table)

    slot = interp_index.reshape(2, TAKES)
    slab = slot >> 4
    source = ((slab >> 5) << 3) | (slab & 7)
    slot = ((source << 6) | (((slab >> 3) & 3) << 4) | (slot & 15)).astype(jnp.float32)
    taps = jnp.concatenate([slot.reshape(8, LANES), interp_frac.reshape(4, LANES)], axis=0)
    weighted = weigh(class_ids, spectra, ctf_table, taps)
    outgoing = outgoing.reshape(32 * N_GRP * 4 * CAP, LANES)
    buffer = exchange(outgoing, ROW_AXES).reshape(32, N_GRP, 4 * CAP, LANES)
    groups = [lax.dynamic_index_in_dim(weighted, here, 0, keepdims=False)]
    for k in range(1, 4):
        block = lax.dynamic_index_in_dim(weighted, (here - k) % 4, 0, keepdims=False)
        groups.append(lax.ppermute(block, "x", [((i + k) % 4, i) for i in range(4)]))
    partial = score(
        (here + turn) % 4,
        buffer,
        jnp.stack(groups),
        own_part(column_table(), "x"),
        jnp.asarray(row_table()),
    )
    total = jnp.sum(exchange(partial, "x"), axis=0)
    orient = 2 * here + jnp.arange(LANES, dtype=jnp.int32) // TRANS
    return jnp.where(orient[None, :] < ori_count[0], total, 0.0)


def solution(mesh):
    fine = Mesh(mesh.devices.reshape(4, 4, 4, 2, 4), SLAB_AXES + ("x",))
    return jax.shard_map(
        shards,
        mesh=fine,
        in_specs=(
            P(SLAB_AXES, "x", None),
            P(SLAB_AXES, "x", None, None),
            P(None, SLAB_AXES, None, "x"),
            P(SLAB_AXES, None, "x"),
            P(SLAB_AXES),
            P(SLAB_AXES, "x", None),
            P(SLAB_AXES),
            P(None, "x", None),
        ),
        out_specs=P(SLAB_AXES, "x"),
        check_vma=False,
    )
```

```python
import math

import jax
import jax.numpy as jnp
import ml_dtypes
import numpy as np
from jax import lax
from jax.experimental import pallas as pl
from jax.experimental.pallas import tpu as pltpu
from jax.sharding import Mesh
from jax.sharding import PartitionSpec as P

NF = 256
CAP = 16
ORI_MAX = 8
TSIDE = 8
PART_DEV = 8
TRANS = 64
N_GRP = 4
COLS = NF // N_GRP
LANES = 2 * COLS
SLAB_ROWS = 512
SLOTS = 2048
TAKES = ORI_MAX * COLS
PARTICLE_ROWS = PART_DEV * COLS
MIX_STEP = 256
EXTRA_ROWS = 32
VMEM_BYTES = 48 * 1024 * 1024
SLAB_AXES = ("y", "h", "l", "c")
ROW_AXES = ("y", "l", "c")


def split_bf16(values):
    high = values.astype(ml_dtypes.bfloat16)
    low = (values - high.astype(np.float64)).astype(ml_dtypes.bfloat16)
    return high, low


def fourier_tables():
    index = np.arange(NF)
    kz = index.reshape(4, 4, 8, 2).transpose(0, 2, 3, 1).reshape(NF)
    angle = 2.0 * math.pi / NF * ((kz[:, None] * index[None, :]) % NF)
    table = np.concatenate([np.cos(angle), np.sin(angle)], axis=1) / math.sqrt(NF)
    return np.stack(split_bf16(table))


def column_table():
    b = np.arange(TRANS) % TSIDE - TSIDE // 2
    v = np.arange(NF)
    angle = -2.0 * math.pi / NF * ((b[None, :] * v[:, None]) % NF)
    fr = np.cos(angle).reshape(N_GRP, COLS, TRANS) / NF
    fi = np.sin(angle).reshape(N_GRP, COLS, TRANS) / NF
    with_er = np.concatenate([fr, fr, -fi, fi], axis=1)
    with_ei = np.concatenate([-fi, -fi, -fr, fr], axis=1)
    high, low = split_bf16(np.concatenate([with_er, with_ei], axis=2))
    return np.concatenate([high, low], axis=2)


def row_table():
    a = np.arange(TRANS) // TSIDE - TSIDE // 2
    u = np.arange(NF)
    angle = -2.0 * math.pi / NF * ((a[None, :] * u[:, None]) % NF)
    table = np.concatenate([np.cos(angle), np.sin(angle)], axis=1).astype(np.float32)
    return table.reshape(N_GRP, COLS, 2 * TRANS)


def down_rows(row):
    return jnp.broadcast_to(row, (LANES, LANES)).T


def hit_tiles(rows, total, weights=(1.0,)):
    lane = lax.broadcasted_iota(jnp.int32, (LANES, LANES), 1).astype(jnp.float32)
    ahead = [down_rows(row) - lane for row in rows]
    tiles = []
    for first in range(0, total, LANES):
        parts = [jnp.where(far == float(first), w, 0.0) for far, w in zip(ahead, weights)]
        tiles.append(sum(parts[1:], parts[0]).astype(jnp.bfloat16))
    return tiles


def fourier_kernel(x_ref, table_ref, out_ref, wide):
    contract = (((1,), (1,)), ((), ()))
    for ky in range(2):
        lines = x_ref[ky]
        turned = jnp.concatenate([lines[:, NF:], -lines[:, :NF]], axis=1)
        both = jnp.concatenate([lines, turned], axis=0)
        high = both.astype(jnp.bfloat16)
        low = (both - high.astype(jnp.float32)).astype(jnp.bfloat16)

        def product(table, part):
            return lax.dot_general(table, part, contract, preferred_element_type=jnp.float32)

        result = (product(table_ref[0], low) + product(table_ref[1], high)) + product(
            table_ref[0], high
        )
        wide[pl.ds(ky, NF, stride=2), :] = result
    rest = 2 * NF // 4
    for y in range(4):
        block = wide[y * rest : (y + 1) * rest, :].astype(jnp.bfloat16)
        for h in range(4):
            out_ref[(y * 4 + h) * rest : (y * 4 + h + 1) * rest, :] = block


def fourier(pencils, table):
    return pl.pallas_call(
        fourier_kernel,
        out_shape=jax.ShapeDtypeStruct((8 * NF, LANES), jnp.bfloat16),
        scratch_shapes=[pltpu.VMEM((2 * NF, LANES), jnp.float32)],
        compiler_params=pltpu.CompilerParams(vmem_limit_bytes=VMEM_BYTES),
        cost_estimate=pl.CostEstimate(
            flops=6 * NF * NF * 2 * NF, bytes_accessed=1 << 20, transcendentals=0
        ),
    )(pencils, table)


def weigh_kernel(class_ref, spectra_ref, ctf_ref, taps_ref, out_ref):
    for particle in range(PART_DEV):
        factor = ctf_ref[class_ref[particle]].astype(jnp.float32)
        lines = spectra_ref[particle].astype(jnp.float32)
        real = lines[:, :NF] * factor
        imag = lines[:, NF:] * factor
        for part in range(N_GRP):
            span = slice(part * COLS, (part + 1) * COLS)
            out_ref[part, particle * COLS : (particle + 1) * COLS, :] = jnp.concatenate(
                [real[:, span], imag[:, span]], axis=1
            ).astype(jnp.bfloat16)
    taps = taps_ref[...]
    place = taps[:8]
    place_high = jnp.floor(place * (1.0 / 16.0))
    place_low = place - 16.0 * place_high
    frac = taps[8:12]
    first = frac.astype(jnp.bfloat16).astype(jnp.float32)
    second = (frac - first).astype(jnp.bfloat16).astype(jnp.float32)
    third = frac - first - second
    extra = jnp.concatenate(
        [place_high, place_low, first, second, third, jnp.zeros_like(frac)], axis=0
    ).astype(jnp.bfloat16)
    for part in range(N_GRP):
        out_ref[part, PARTICLE_ROWS:, :] = extra


def weigh(class_ids, spectra, ctf_table, taps):
    vmem = pl.BlockSpec(memory_space=pltpu.VMEM)
    return pl.pallas_call(
        weigh_kernel,
        in_specs=[pl.BlockSpec(memory_space=pltpu.SMEM)] + [vmem] * 3,
        out_specs=vmem,
        out_shape=jax.ShapeDtypeStruct((N_GRP, PARTICLE_ROWS + EXTRA_ROWS, LANES), jnp.bfloat16),
        compiler_params=pltpu.CompilerParams(vmem_limit_bytes=VMEM_BYTES),
        cost_estimate=pl.CostEstimate(flops=1 << 20, bytes_accessed=2 << 20, transcendentals=0),
    )(class_ids, spectra, ctf_table, taps)


def pick_kernel(order_ref, place_ref, table_ref, out_ref, wide, slabs, hits):
    del order_ref

    @pl.when(pl.program_id(0) == 0)
    def _():
        wide[...] = table_ref[...].astype(jnp.float32)
        for slab in range(4):
            for ky in range(2):
                slabs[slab, ky * NF : (ky + 1) * NF, :] = wide[
                    pl.ds(2 * slab + ky, NF, stride=8), :
                ].astype(jnp.bfloat16)

    for slab in range(4):
        for row in range(4):
            tiles = hit_tiles([place_ref[slab, row : row + 1, :]], SLAB_ROWS)
            for at, tile in enumerate(tiles):
                hits[row * LANES : (row + 1) * LANES, at * LANES : (at + 1) * LANES] = tile
        taken = jnp.dot(hits[...], slabs[slab], preferred_element_type=jnp.float32)
        out_ref[:, slab, :, :] = taken.astype(jnp.bfloat16).reshape(32, CAP, LANES)


def pick(order, place, table):
    return pl.pallas_call(
        pick_kernel,
        grid_spec=pltpu.PrefetchScalarGridSpec(
            num_scalar_prefetch=1,
            grid=(N_GRP,),
            in_specs=[
                pl.BlockSpec((4, None, 4, LANES), lambda i, order: (0, i, 0, 0)),
                pl.BlockSpec((4 * SLAB_ROWS, LANES), lambda i, order: (0, 0)),
            ],
            out_specs=pl.BlockSpec(
                (32, None, 4, CAP, LANES), lambda i, order: (0, order[i], 0, 0, 0)
            ),
            scratch_shapes=[
                pltpu.VMEM((4 * SLAB_ROWS, LANES), jnp.float32),
                pltpu.VMEM((4, SLAB_ROWS, LANES), jnp.bfloat16),
                pltpu.VMEM((SLAB_ROWS, SLAB_ROWS), jnp.bfloat16),
            ],
        ),
        out_shape=pltpu.HBM((32, N_GRP, 4, CAP, LANES), jnp.bfloat16),
        compiler_params=pltpu.CompilerParams(vmem_limit_bytes=VMEM_BYTES),
        cost_estimate=pl.CostEstimate(
            flops=16 * SLOTS * SLAB_ROWS * LANES, bytes_accessed=4 << 20, transcendentals=0
        ),
    )(order, place, table)


def score_kernel(order_ref, buffer_ref, weighted_ref, col_ref, row_ref, out_ref, slices):
    del order_ref
    extra = weighted_ref[PARTICLE_ROWS:, :].astype(jnp.float32)
    place = 16.0 * extra[:8] + extra[8:16]
    frac = extra[16:20] + extra[20:24] + extra[24:28]
    lane = lax.broadcasted_iota(jnp.int32, (LANES, LANES), 1).astype(jnp.float32)
    takes = []
    for row in range(4):
        share = down_rows(frac[row : row + 1])
        takes.append(
            (
                down_rows(place[row : row + 1]) - lane,
                1.0 - share,
                down_rows(place[row + 4 : row + 5]) - lane,
                share,
            )
        )
    rows = buffer_ref[...].reshape(SLOTS, LANES)
    mixed = None
    for start in range(0, SLOTS, MIX_STEP):
        blocks = [
            jnp.concatenate(
                [
                    (
                        jnp.where(far == float(first), rest, 0.0)
                        + jnp.where(far_next == float(first), share, 0.0)
                    ).astype(jnp.bfloat16)
                    for first in range(start, start + MIX_STEP, LANES)
                ],
                axis=1,
            )
            for far, rest, far_next, share in takes
        ]
        part = jnp.dot(
            jnp.concatenate(blocks, axis=0),
            rows[start : start + MIX_STEP],
            preferred_element_type=jnp.float32,
        )
        mixed = part if mixed is None else mixed + part
    slices[...] = mixed
    phase_rows = row_ref[...]
    left = lax.broadcasted_iota(jnp.int32, (PART_DEV, LANES), 1) < TRANS
    weight = weighted_ref[:PARTICLE_ROWS, :].astype(jnp.float32).reshape(PART_DEV, COLS, LANES)
    for pair in range(ORI_MAX // 2):
        products = []
        for orient in (2 * pair, 2 * pair + 1):
            plain = slices[orient * COLS : (orient + 1) * COLS, :]
            swapped = pltpu.roll(plain, COLS, 1)
            products.append(
                jnp.concatenate(
                    [
                        (weight * plain[None]).astype(jnp.bfloat16),
                        (weight * swapped[None]).astype(jnp.bfloat16),
                    ],
                    axis=-1,
                ).reshape(PARTICLE_ROWS, 2 * LANES)
            )
        columns = jnp.dot(
            jnp.concatenate(products, axis=0), col_ref[...], preferred_element_type=jnp.float32
        )
        columns = (columns[:, :LANES] + columns[:, LANES:]).reshape(2, PART_DEV, COLS, LANES)
        summed = jnp.sum(columns * phase_rows[None, None], axis=2)
        done = [summed[at] + pltpu.roll(summed[at], TRANS, 1) for at in range(2)]
        total = jnp.where(left, done[0], done[1])

        @pl.when(pl.program_id(0) == 0)
        def _():
            out_ref[pair] = total

        @pl.when(pl.program_id(0) > 0)
        def _():
            out_ref[pair] += total


def score(order, buffer, weighted, col_phase, row_phase):
    return pl.pallas_call(
        score_kernel,
        grid_spec=pltpu.PrefetchScalarGridSpec(
            num_scalar_prefetch=1,
            grid=(N_GRP,),
            in_specs=[
                pl.BlockSpec(
                    (32, None, 4 * CAP, LANES), lambda i, order: (0, order[i], 0, 0)
                ),
                pl.BlockSpec(
                    (None, PARTICLE_ROWS + EXTRA_ROWS, LANES), lambda i, order: (i, 0, 0)
                ),
                pl.BlockSpec((2 * LANES, 2 * LANES), lambda i, order: (0, 0)),
                pl.BlockSpec((None, COLS, LANES), lambda i, order: (order[i], 0, 0)),
            ],
            out_specs=pl.BlockSpec(
                (ORI_MAX // 2, PART_DEV, LANES), lambda i, order: (0, 0, 0)
            ),
            scratch_shapes=[
                pltpu.VMEM((TAKES, LANES), jnp.float32),
            ],
        ),
        out_shape=jax.ShapeDtypeStruct((ORI_MAX // 2, PART_DEV, LANES), jnp.float32),
        compiler_params=pltpu.CompilerParams(vmem_limit_bytes=VMEM_BYTES),
        cost_estimate=pl.CostEstimate(flops=8 << 30, bytes_accessed=4 << 20, transcendentals=0),
    )(order, buffer, weighted, col_phase, row_phase)


def exchange(values, axes):
    return lax.all_to_all(values, axes, split_axis=0, concat_axis=0, tiled=True)


def own_part(table, axis):
    return lax.dynamic_index_in_dim(jnp.asarray(table), lax.axis_index(axis), 0, keepdims=False)


def shards(pencils, send_map, interp_index, interp_frac, ori_count, spectra, class_ids, ctf_table):
    here = lax.axis_index("x")
    turn = jnp.arange(4, dtype=jnp.int32)
    table = exchange(fourier(pencils, jnp.asarray(fourier_tables())), SLAB_AXES)

    wanted = jnp.maximum(send_map[0, 0], 0)
    place = ((wanted & 1) << 8) | (wanted & (NF - 2)) | (wanted >> 8)
    place = place.astype(jnp.float32).reshape(4, 4, 8, CAP).transpose(1, 0, 2, 3)
    place = place.reshape(4, 4, LANES)
    maps = [place] + [
        lax.ppermute(place, "x", [((i + k) % 4, i) for i in range(4)]) for k in range(1, 4)
    ]
    maps = lax.all_gather(jnp.stack(maps), "h", axis=0)
    maps = lax.dynamic_index_in_dim(maps, lax.axis_index("h"), 2, keepdims=False)
    outgoing = pick((here + turn) % 4, maps, table)

    slot = interp_index.reshape(2, TAKES)
    slab = slot >> 4
    source = ((slab >> 5) << 3) | (slab & 7)
    slot = ((source << 6) | (((slab >> 3) & 3) << 4) | (slot & 15)).astype(jnp.float32)
    taps = jnp.concatenate([slot.reshape(8, LANES), interp_frac.reshape(4, LANES)], axis=0)
    weighted = weigh(class_ids, spectra, ctf_table, taps)
    outgoing = outgoing.reshape(32 * N_GRP * 4 * CAP, LANES)
    buffer = exchange(outgoing, ROW_AXES).reshape(32, N_GRP, 4 * CAP, LANES)
    groups = [lax.dynamic_index_in_dim(weighted, here, 0, keepdims=False)]
    for k in range(1, 4):
        block = lax.dynamic_index_in_dim(weighted, (here - k) % 4, 0, keepdims=False)
        groups.append(lax.ppermute(block, "x", [((i + k) % 4, i) for i in range(4)]))
    partial = score(
        (here + turn) % 4,
        buffer,
        jnp.stack(groups),
        own_part(column_table(), "x"),
        jnp.asarray(row_table()),
    )
    total = jnp.sum(exchange(partial, "x"), axis=0)
    orient = 2 * here + jnp.arange(LANES, dtype=jnp.int32) // TRANS
    return jnp.where(orient[None, :] < ori_count[0], total, 0.0)


def solution(mesh):
    fine = Mesh(mesh.devices.reshape(4, 4, 4, 2, 4), SLAB_AXES + ("x",))
    return jax.shard_map(
        shards,
        mesh=fine,
        in_specs=(
            P(SLAB_AXES, "x", None),
            P(SLAB_AXES, "x", None, None),
            P(None, SLAB_AXES, None, "x"),
            P(SLAB_AXES, None, "x"),
            P(SLAB_AXES),
            P(SLAB_AXES, "x", None),
            P(SLAB_AXES),
            P(None, "x", None),
        ),
        out_specs=P(SLAB_AXES, "x"),
        check_vma=False,
    )
```

```python
import math

import jax
import jax.numpy as jnp
import ml_dtypes
import numpy as np
from jax import lax
from jax.experimental import pallas as pl
from jax.experimental.pallas import tpu as pltpu
from jax.sharding import Mesh
from jax.sharding import PartitionSpec as P

NF = 256
CAP = 16
ORI_MAX = 8
TSIDE = 8
PART_DEV = 8
TRANS = 64
N_GRP = 4
COLS = NF // N_GRP
LANES = 2 * COLS
SLAB_ROWS = 512
SLOTS = 2048
TAKES = ORI_MAX * COLS
PARTICLE_ROWS = PART_DEV * COLS
MIX_STEP = 256
EXTRA_ROWS = 32
VMEM_BYTES = 48 * 1024 * 1024
SLAB_AXES = ("y", "h", "l", "c")
ROW_AXES = ("y", "l", "c")


def split_bf16(values):
    high = values.astype(ml_dtypes.bfloat16)
    low = (values - high.astype(np.float64)).astype(ml_dtypes.bfloat16)
    return high, low


def fourier_tables():
    index = np.arange(NF)
    kz = index.reshape(4, 4, 8, 2).transpose(0, 2, 3, 1).reshape(NF)
    angle = 2.0 * math.pi / NF * ((kz[:, None] * index[None, :]) % NF)
    table = np.concatenate([np.cos(angle), np.sin(angle)], axis=1) / math.sqrt(NF)
    return np.stack(split_bf16(table))


def column_table():
    t = np.arange(TRANS)
    a = t // TSIDE - TSIDE // 2
    b = t % TSIDE - TSIDE // 2
    v = np.arange(NF).reshape(N_GRP, 1, COLS, 1)
    d = np.arange(8).reshape(1, 8, 1, 1)
    angle = -2.0 * math.pi / NF * ((b * v + 8 * a * d) % NF)
    fr = np.cos(angle) / NF
    fi = np.sin(angle) / NF
    with_er = np.concatenate([fr, fr, -fi, fi], axis=2)
    with_ei = np.concatenate([-fi, -fi, -fr, fr], axis=2)
    high, low = split_bf16(np.concatenate([with_er, with_ei], axis=3))
    return np.concatenate([high, low], axis=3)


def row_table():
    a = np.arange(TRANS) // TSIDE - TSIDE // 2
    u = np.arange(NF).reshape(N_GRP, COLS)[:, :8]
    angle = -2.0 * math.pi / NF * ((a * u[:, :, None]) % NF)
    return np.concatenate([np.cos(angle), np.sin(angle)], axis=2).astype(np.float32)


def down_rows(row):
    return jnp.broadcast_to(row, (LANES, LANES)).T


def hit_tiles(rows, total, weights=(1.0,)):
    lane = lax.broadcasted_iota(jnp.int32, (LANES, LANES), 1).astype(jnp.float32)
    ahead = [down_rows(row) - lane for row in rows]
    tiles = []
    for first in range(0, total, LANES):
        parts = [jnp.where(far == float(first), w, 0.0) for far, w in zip(ahead, weights)]
        tiles.append(sum(parts[1:], parts[0]).astype(jnp.bfloat16))
    return tiles


def fourier_kernel(x_ref, table_ref, out_ref, wide):
    contract = (((1,), (1,)), ((), ()))
    for ky in range(2):
        lines = x_ref[ky]
        turned = jnp.concatenate([lines[:, NF:], -lines[:, :NF]], axis=1)
        both = jnp.concatenate([lines, turned], axis=0)
        high = both.astype(jnp.bfloat16)
        low = (both - high.astype(jnp.float32)).astype(jnp.bfloat16)

        def product(table, part):
            return lax.dot_general(table, part, contract, preferred_element_type=jnp.float32)

        result = (product(table_ref[0], low) + product(table_ref[1], high)) + product(
            table_ref[0], high
        )
        wide[pl.ds(ky, NF, stride=2), :] = result
    rest = 2 * NF // 4
    for y in range(4):
        block = wide[y * rest : (y + 1) * rest, :].astype(jnp.bfloat16)
        for h in range(4):
            out_ref[(y * 4 + h) * rest : (y * 4 + h + 1) * rest, :] = block


def fourier(pencils, table):
    return pl.pallas_call(
        fourier_kernel,
        out_shape=jax.ShapeDtypeStruct((8 * NF, LANES), jnp.bfloat16),
        scratch_shapes=[pltpu.VMEM((2 * NF, LANES), jnp.float32)],
        compiler_params=pltpu.CompilerParams(vmem_limit_bytes=VMEM_BYTES),
        cost_estimate=pl.CostEstimate(
            flops=6 * NF * NF * 2 * NF, bytes_accessed=1 << 20, transcendentals=0
        ),
    )(pencils, table)


def weigh_kernel(class_ref, spectra_ref, ctf_ref, taps_ref, out_ref):
    for particle in range(PART_DEV):
        factor = ctf_ref[class_ref[particle]].astype(jnp.float32)
        lines = spectra_ref[particle].astype(jnp.float32)
        real = lines[:, :NF] * factor
        imag = lines[:, NF:] * factor
        for part in range(N_GRP):
            span = slice(part * COLS, (part + 1) * COLS)
            out_ref[part, particle * COLS : (particle + 1) * COLS, :] = jnp.concatenate(
                [real[:, span], imag[:, span]], axis=1
            ).astype(jnp.bfloat16)
    taps = taps_ref[...]
    place = taps[:8]
    place_high = jnp.floor(place * (1.0 / 16.0))
    place_low = place - 16.0 * place_high
    frac = taps[8:12]
    first = frac.astype(jnp.bfloat16).astype(jnp.float32)
    second = (frac - first).astype(jnp.bfloat16).astype(jnp.float32)
    third = frac - first - second
    extra = jnp.concatenate(
        [place_high, place_low, first, second, third, jnp.zeros_like(frac)], axis=0
    ).astype(jnp.bfloat16)
    for part in range(N_GRP):
        out_ref[part, PARTICLE_ROWS:, :] = extra


def weigh(class_ids, spectra, ctf_table, taps):
    vmem = pl.BlockSpec(memory_space=pltpu.VMEM)
    return pl.pallas_call(
        weigh_kernel,
        in_specs=[pl.BlockSpec(memory_space=pltpu.SMEM)] + [vmem] * 3,
        out_specs=vmem,
        out_shape=jax.ShapeDtypeStruct((N_GRP, PARTICLE_ROWS + EXTRA_ROWS, LANES), jnp.bfloat16),
        compiler_params=pltpu.CompilerParams(vmem_limit_bytes=VMEM_BYTES),
        cost_estimate=pl.CostEstimate(flops=1 << 20, bytes_accessed=2 << 20, transcendentals=0),
    )(class_ids, spectra, ctf_table, taps)


def pick_kernel(order_ref, place_ref, table_ref, out_ref, wide, slabs, hits):
    del order_ref

    @pl.when(pl.program_id(0) == 0)
    def _():
        wide[...] = table_ref[...].astype(jnp.float32)
        for slab in range(4):
            for ky in range(2):
                slabs[slab, ky * NF : (ky + 1) * NF, :] = wide[
                    pl.ds(2 * slab + ky, NF, stride=8), :
                ].astype(jnp.bfloat16)

    for slab in range(4):
        for row in range(4):
            tiles = hit_tiles([place_ref[slab, row : row + 1, :]], SLAB_ROWS)
            for at, tile in enumerate(tiles):
                hits[row * LANES : (row + 1) * LANES, at * LANES : (at + 1) * LANES] = tile
        taken = jnp.dot(hits[...], slabs[slab], preferred_element_type=jnp.float32)
        out_ref[:, slab, :, :] = taken.astype(jnp.bfloat16).reshape(32, CAP, LANES)


def pick(order, place, table):
    return pl.pallas_call(
        pick_kernel,
        grid_spec=pltpu.PrefetchScalarGridSpec(
            num_scalar_prefetch=1,
            grid=(N_GRP,),
            in_specs=[
                pl.BlockSpec((4, None, 4, LANES), lambda i, order: (0, i, 0, 0)),
                pl.BlockSpec((4 * SLAB_ROWS, LANES), lambda i, order: (0, 0)),
            ],
            out_specs=pl.BlockSpec(
                (32, None, 4, CAP, LANES), lambda i, order: (0, order[i], 0, 0, 0)
            ),
            scratch_shapes=[
                pltpu.VMEM((4 * SLAB_ROWS, LANES), jnp.float32),
                pltpu.VMEM((4, SLAB_ROWS, LANES), jnp.bfloat16),
                pltpu.VMEM((SLAB_ROWS, SLAB_ROWS), jnp.bfloat16),
            ],
        ),
        out_shape=pltpu.HBM((32, N_GRP, 4, CAP, LANES), jnp.bfloat16),
        compiler_params=pltpu.CompilerParams(vmem_limit_bytes=VMEM_BYTES),
        cost_estimate=pl.CostEstimate(
            flops=16 * SLOTS * SLAB_ROWS * LANES, bytes_accessed=4 << 20, transcendentals=0
        ),
    )(order, place, table)


def score_kernel(order_ref, buffer_ref, weighted_ref, col_ref, row_ref, out_ref, slices):
    del order_ref
    extra = weighted_ref[PARTICLE_ROWS:, :].astype(jnp.float32)
    place = 16.0 * extra[:8] + extra[8:16]
    frac = extra[16:20] + extra[20:24] + extra[24:28]
    lane = lax.broadcasted_iota(jnp.int32, (LANES, LANES), 1).astype(jnp.float32)
    takes = []
    for row in range(4):
        share = down_rows(frac[row : row + 1])
        takes.append(
            (
                down_rows(place[row : row + 1]) - lane,
                1.0 - share,
                down_rows(place[row + 4 : row + 5]) - lane,
                share,
            )
        )
    rows = buffer_ref[...].reshape(SLOTS, LANES)
    mixed = None
    for start in range(0, SLOTS, MIX_STEP):
        blocks = [
            jnp.concatenate(
                [
                    (
                        jnp.where(far == float(first), rest, 0.0)
                        + jnp.where(far_next == float(first), share, 0.0)
                    ).astype(jnp.bfloat16)
                    for first in range(start, start + MIX_STEP, LANES)
                ],
                axis=1,
            )
            for far, rest, far_next, share in takes
        ]
        part = jnp.dot(
            jnp.concatenate(blocks, axis=0),
            rows[start : start + MIX_STEP],
            preferred_element_type=jnp.float32,
        )
        mixed = part if mixed is None else mixed + part
    slices[...] = mixed
    plain = slices[...]
    plain_parts = plain.reshape(ORI_MAX, 1, 8, 8, LANES)
    swapped_parts = pltpu.roll(plain, COLS, 1).reshape(ORI_MAX, 1, 8, 8, LANES)
    weight = weighted_ref[:PARTICLE_ROWS, :].astype(jnp.float32)
    weight = weight.reshape(1, PART_DEV, 8, 8, LANES)
    columns = None
    for d in range(8):
        products = jnp.concatenate(
            [
                (weight[:, :, d] * parts[:, :, d]).reshape(8 * COLS, LANES).astype(jnp.bfloat16)
                for parts in (plain_parts, swapped_parts)
            ],
            axis=1,
        )
        part = jnp.dot(products, col_ref[d], preferred_element_type=jnp.float32)
        columns = part if columns is None else columns + part
    columns = (columns[:, :LANES] + columns[:, LANES:]).reshape(ORI_MAX * PART_DEV, 8, LANES)
    summed = jnp.sum(columns * row_ref[...][None], axis=1)
    folded = (summed + pltpu.roll(summed, TRANS, 1)).reshape(ORI_MAX // 2, 2, PART_DEV, LANES)
    left = lax.broadcasted_iota(jnp.int32, (ORI_MAX // 2, PART_DEV, LANES), 2) < TRANS
    total = jnp.where(left, folded[:, 0], folded[:, 1])

    @pl.when(pl.program_id(0) == 0)
    def _():
        out_ref[...] = total

    @pl.when(pl.program_id(0) > 0)
    def _():
        out_ref[...] += total


def score(order, buffer, weighted, col_phase, row_phase):
    return pl.pallas_call(
        score_kernel,
        grid_spec=pltpu.PrefetchScalarGridSpec(
            num_scalar_prefetch=1,
            grid=(N_GRP,),
            in_specs=[
                pl.BlockSpec(
                    (32, None, 4 * CAP, LANES), lambda i, order: (0, order[i], 0, 0)
                ),
                pl.BlockSpec(
                    (None, PARTICLE_ROWS + EXTRA_ROWS, LANES), lambda i, order: (i, 0, 0)
                ),
                pl.BlockSpec((8, 2 * LANES, 2 * LANES), lambda i, order: (0, 0, 0)),
                pl.BlockSpec((None, 8, LANES), lambda i, order: (order[i], 0, 0)),
            ],
            out_specs=pl.BlockSpec(
                (ORI_MAX // 2, PART_DEV, LANES), lambda i, order: (0, 0, 0)
            ),
            scratch_shapes=[
                pltpu.VMEM((TAKES, LANES), jnp.float32),
            ],
        ),
        out_shape=jax.ShapeDtypeStruct((ORI_MAX // 2, PART_DEV, LANES), jnp.float32),
        compiler_params=pltpu.CompilerParams(vmem_limit_bytes=VMEM_BYTES),
        cost_estimate=pl.CostEstimate(flops=8 << 30, bytes_accessed=4 << 20, transcendentals=0),
    )(order, buffer, weighted, col_phase, row_phase)


def exchange(values, axes):
    return lax.all_to_all(values, axes, split_axis=0, concat_axis=0, tiled=True)


def own_part(table, axis):
    return lax.dynamic_index_in_dim(jnp.asarray(table), lax.axis_index(axis), 0, keepdims=False)


def shards(pencils, send_map, interp_index, interp_frac, ori_count, spectra, class_ids, ctf_table):
    here = lax.axis_index("x")
    turn = jnp.arange(4, dtype=jnp.int32)
    table = exchange(fourier(pencils, jnp.asarray(fourier_tables())), SLAB_AXES)

    wanted = jnp.maximum(send_map[0, 0], 0)
    place = ((wanted & 1) << 8) | (wanted & (NF - 2)) | (wanted >> 8)
    place = place.astype(jnp.float32).reshape(4, 4, 8, CAP).transpose(1, 0, 2, 3)
    place = place.reshape(4, 4, LANES)
    maps = [place] + [
        lax.ppermute(place, "x", [((i + k) % 4, i) for i in range(4)]) for k in range(1, 4)
    ]
    maps = lax.all_gather(jnp.stack(maps), "h", axis=0)
    maps = lax.dynamic_index_in_dim(maps, lax.axis_index("h"), 2, keepdims=False)
    outgoing = pick((here + turn) % 4, maps, table)

    slot = interp_index.reshape(2, TAKES)
    slab = slot >> 4
    source = ((slab >> 5) << 3) | (slab & 7)
    slot = ((source << 6) | (((slab >> 3) & 3) << 4) | (slot & 15)).astype(jnp.float32)
    taps = jnp.concatenate([slot.reshape(8, LANES), interp_frac.reshape(4, LANES)], axis=0)
    weighted = weigh(class_ids, spectra, ctf_table, taps)
    outgoing = outgoing.reshape(32 * N_GRP * 4 * CAP, LANES)
    buffer = exchange(outgoing, ROW_AXES).reshape(32, N_GRP, 4 * CAP, LANES)
    groups = [lax.dynamic_index_in_dim(weighted, here, 0, keepdims=False)]
    for k in range(1, 4):
        block = lax.dynamic_index_in_dim(weighted, (here - k) % 4, 0, keepdims=False)
        groups.append(lax.ppermute(block, "x", [((i + k) % 4, i) for i in range(4)]))
    partial = score(
        (here + turn) % 4,
        buffer,
        jnp.stack(groups),
        own_part(column_table(), "x"),
        jnp.asarray(row_table()),
    )
    total = jnp.sum(exchange(partial, "x"), axis=0)
    orient = 2 * here + jnp.arange(LANES, dtype=jnp.int32) // TRANS
    return jnp.where(orient[None, :] < ori_count[0], total, 0.0)


def solution(mesh):
    fine = Mesh(mesh.devices.reshape(4, 4, 4, 2, 4), SLAB_AXES + ("x",))
    return jax.shard_map(
        shards,
        mesh=fine,
        in_specs=(
            P(SLAB_AXES, "x", None),
            P(SLAB_AXES, "x", None, None),
            P(None, SLAB_AXES, None, "x"),
            P(SLAB_AXES, None, "x"),
            P(SLAB_AXES),
            P(SLAB_AXES, "x", None),
            P(SLAB_AXES),
            P(None, "x", None),
        ),
        out_specs=P(SLAB_AXES, "x"),
        check_vma=False,
    )
```

```python
import math

import jax
import jax.numpy as jnp
import ml_dtypes
import numpy as np
from jax import lax
from jax.experimental import pallas as pl
from jax.experimental.pallas import tpu as pltpu
from jax.sharding import Mesh
from jax.sharding import PartitionSpec as P

NF = 256
CAP = 16
ORI_MAX = 8
TSIDE = 8
PART_DEV = 8
TRANS = 64
N_GRP = 4
COLS = NF // N_GRP
LANES = 2 * COLS
SLAB_ROWS = 512
SLOTS = 2048
TAKES = ORI_MAX * COLS
PARTICLE_ROWS = PART_DEV * COLS
MIX_STEP = 256
EXTRA_ROWS = 32
VMEM_BYTES = 48 * 1024 * 1024
SLAB_AXES = ("y", "h", "l", "c")
ROW_AXES = ("y", "l", "c")


def split_bf16(values):
    high = values.astype(ml_dtypes.bfloat16)
    low = (values - high.astype(np.float64)).astype(ml_dtypes.bfloat16)
    return high, low


def fourier_tables():
    index = np.arange(NF)
    kz = index.reshape(4, 4, 8, 2).transpose(0, 2, 3, 1).reshape(NF)
    angle = 2.0 * math.pi / NF * ((kz[:, None] * index[None, :]) % NF)
    table = np.concatenate([np.cos(angle), np.sin(angle)], axis=1) / math.sqrt(NF)
    return np.stack(split_bf16(table))


def column_table():
    t = np.arange(TRANS)
    a = t // TSIDE - TSIDE // 2
    b = t % TSIDE - TSIDE // 2
    v = np.arange(NF).reshape(N_GRP, 1, COLS, 1)
    d = np.arange(8).reshape(1, 8, 1, 1)
    angle = -2.0 * math.pi / NF * ((b * v + 8 * a * d) % NF)
    fr = np.cos(angle) / NF
    fi = np.sin(angle) / NF
    with_er = np.concatenate([fr, fr, -fi, fi], axis=2)
    with_ei = np.concatenate([-fi, -fi, -fr, fr], axis=2)
    high, low = split_bf16(np.concatenate([with_er, with_ei], axis=3))
    return np.concatenate([high, low], axis=3)


def row_table():
    a = np.arange(TRANS) // TSIDE - TSIDE // 2
    u = np.arange(NF).reshape(N_GRP, COLS)[:, :8]
    angle = -2.0 * math.pi / NF * ((a * u[:, :, None]) % NF)
    return np.concatenate([np.cos(angle), np.sin(angle)], axis=2).astype(np.float32)


def down_rows(row):
    return jnp.broadcast_to(row, (LANES, LANES)).T


def fourier_kernel(x_ref, table_ref, out_ref, wide):
    contract = (((1,), (1,)), ((), ()))
    for ky in range(2):
        lines = x_ref[ky]
        turned = jnp.concatenate([lines[:, NF:], -lines[:, :NF]], axis=1)
        both = jnp.concatenate([lines, turned], axis=0)
        high = both.astype(jnp.bfloat16)
        low = (both - high.astype(jnp.float32)).astype(jnp.bfloat16)

        def product(table, part):
            return lax.dot_general(table, part, contract, preferred_element_type=jnp.float32)

        result = (product(table_ref[0], low) + product(table_ref[1], high)) + product(
            table_ref[0], high
        )
        wide[pl.ds(ky, NF, stride=2), :] = result
    rest = 2 * NF // 4
    for y in range(4):
        block = wide[y * rest : (y + 1) * rest, :].astype(jnp.bfloat16)
        for h in range(4):
            out_ref[(y * 4 + h) * rest : (y * 4 + h + 1) * rest, :] = block


def fourier(pencils, table):
    return pl.pallas_call(
        fourier_kernel,
        out_shape=jax.ShapeDtypeStruct((8 * NF, LANES), jnp.bfloat16),
        scratch_shapes=[pltpu.VMEM((2 * NF, LANES), jnp.float32)],
        compiler_params=pltpu.CompilerParams(vmem_limit_bytes=VMEM_BYTES),
        cost_estimate=pl.CostEstimate(
            flops=6 * NF * NF * 2 * NF, bytes_accessed=1 << 20, transcendentals=0
        ),
    )(pencils, table)


def weigh_kernel(class_ref, spectra_ref, ctf_ref, taps_ref, out_ref):
    for particle in range(PART_DEV):
        factor = ctf_ref[class_ref[particle]].astype(jnp.float32)
        lines = spectra_ref[particle].astype(jnp.float32)
        real = lines[:, :NF] * factor
        imag = lines[:, NF:] * factor
        for part in range(N_GRP):
            span = slice(part * COLS, (part + 1) * COLS)
            out_ref[part, particle * COLS : (particle + 1) * COLS, :] = jnp.concatenate(
                [real[:, span], imag[:, span]], axis=1
            ).astype(jnp.bfloat16)
    taps = taps_ref[...]
    place = taps[:8]
    place_high = jnp.floor(place * (1.0 / 16.0))
    place_low = place - 16.0 * place_high
    frac = taps[8:12]
    first = frac.astype(jnp.bfloat16).astype(jnp.float32)
    second = (frac - first).astype(jnp.bfloat16).astype(jnp.float32)
    third = frac - first - second
    extra = jnp.concatenate(
        [place_high, place_low, first, second, third, jnp.zeros_like(frac)], axis=0
    ).astype(jnp.bfloat16)
    for part in range(N_GRP):
        out_ref[part, PARTICLE_ROWS:, :] = extra


def weigh(class_ids, spectra, ctf_table, taps):
    vmem = pl.BlockSpec(memory_space=pltpu.VMEM)
    return pl.pallas_call(
        weigh_kernel,
        in_specs=[pl.BlockSpec(memory_space=pltpu.SMEM)] + [vmem] * 3,
        out_specs=vmem,
        out_shape=jax.ShapeDtypeStruct((N_GRP, PARTICLE_ROWS + EXTRA_ROWS, LANES), jnp.bfloat16),
        compiler_params=pltpu.CompilerParams(vmem_limit_bytes=VMEM_BYTES),
        cost_estimate=pl.CostEstimate(flops=1 << 20, bytes_accessed=2 << 20, transcendentals=0),
    )(class_ids, spectra, ctf_table, taps)


def pick_kernel(order_ref, place_ref, table_ref, out_ref, wide, slabs, hits):
    del order_ref

    @pl.when(pl.program_id(0) == 0)
    def _():
        wide[...] = table_ref[...].astype(jnp.float32)
        for slab in range(4):
            for ky in range(2):
                slabs[slab, :, ky * LANES : (ky + 1) * LANES] = wide[
                    pl.ds(2 * slab + ky, NF, stride=8), :
                ].astype(jnp.bfloat16)

    lane = lax.broadcasted_iota(jnp.int32, (LANES, LANES), 1).astype(jnp.float32)
    for slab in range(4):
        later = []
        for row in range(4):
            column = down_rows(place_ref[slab, row : row + 1, :])
            later.append(column >= float(NF))
            ahead = jnp.where(later[-1], column - float(NF), column) - lane
            for first in range(0, NF, LANES):
                hits[row * LANES : (row + 1) * LANES, first : first + LANES] = jnp.where(
                    ahead == float(first), 1.0, 0.0
                ).astype(jnp.bfloat16)
        taken = jnp.dot(hits[...], slabs[slab], preferred_element_type=jnp.float32)
        for row in range(4):
            span = taken[row * LANES : (row + 1) * LANES]
            chosen = jnp.where(later[row], span[:, LANES:], span[:, :LANES])
            out_ref[row * 8 : (row + 1) * 8, slab, :, :] = chosen.astype(jnp.bfloat16).reshape(
                8, CAP, LANES
            )


def pick(order, place, table):
    return pl.pallas_call(
        pick_kernel,
        grid_spec=pltpu.PrefetchScalarGridSpec(
            num_scalar_prefetch=1,
            grid=(N_GRP,),
            in_specs=[
                pl.BlockSpec((4, None, 4, LANES), lambda i, order: (0, i, 0, 0)),
                pl.BlockSpec((4 * SLAB_ROWS, LANES), lambda i, order: (0, 0)),
            ],
            out_specs=pl.BlockSpec(
                (32, None, 4, CAP, LANES), lambda i, order: (0, order[i], 0, 0, 0)
            ),
            scratch_shapes=[
                pltpu.VMEM((4 * SLAB_ROWS, LANES), jnp.float32),
                pltpu.VMEM((4, NF, 2 * LANES), jnp.bfloat16),
                pltpu.VMEM((SLAB_ROWS, NF), jnp.bfloat16),
            ],
        ),
        out_shape=pltpu.HBM((32, N_GRP, 4, CAP, LANES), jnp.bfloat16),
        compiler_params=pltpu.CompilerParams(vmem_limit_bytes=VMEM_BYTES),
        cost_estimate=pl.CostEstimate(
            flops=16 * SLOTS * SLAB_ROWS * LANES, bytes_accessed=4 << 20, transcendentals=0
        ),
    )(order, place, table)


def score_kernel(order_ref, buffer_ref, w0, w1, w2, w3, col_ref, row_ref, out_ref, slices, weighted_ref):
    del order_ref
    for at, source in enumerate((w0, w1, w2, w3)):

        @pl.when(pl.program_id(0) == at)
        def _(source=source):
            weighted_ref[...] = source[...]

    extra = weighted_ref[PARTICLE_ROWS:, :].astype(jnp.float32)
    place = 16.0 * extra[:8] + extra[8:16]
    frac = extra[16:20] + extra[20:24] + extra[24:28]
    lane = lax.broadcasted_iota(jnp.int32, (LANES, LANES), 1).astype(jnp.float32)
    takes = []
    for row in range(4):
        share = down_rows(frac[row : row + 1])
        takes.append(
            (
                down_rows(place[row : row + 1]) - lane,
                1.0 - share,
                down_rows(place[row + 4 : row + 5]) - lane,
                share,
            )
        )
    rows = buffer_ref[...].reshape(SLOTS, LANES)
    mixed = None
    for start in range(0, SLOTS, MIX_STEP):
        blocks = [
            jnp.concatenate(
                [
                    (
                        jnp.where(far == float(first), rest, 0.0)
                        + jnp.where(far_next == float(first), share, 0.0)
                    ).astype(jnp.bfloat16)
                    for first in range(start, start + MIX_STEP, LANES)
                ],
                axis=1,
            )
            for far, rest, far_next, share in takes
        ]
        part = jnp.dot(
            jnp.concatenate(blocks, axis=0),
            rows[start : start + MIX_STEP],
            preferred_element_type=jnp.float32,
        )
        mixed = part if mixed is None else mixed + part
    slices[...] = mixed
    plain = slices[...]
    plain_parts = plain.reshape(ORI_MAX, 1, 8, 8, LANES)
    swapped_parts = pltpu.roll(plain, COLS, 1).reshape(ORI_MAX, 1, 8, 8, LANES)
    weight = weighted_ref[:PARTICLE_ROWS, :].astype(jnp.float32)
    weight = weight.reshape(1, PART_DEV, 8, 8, LANES)
    columns = None
    for d in range(8):
        products = jnp.concatenate(
            [
                (weight[:, :, d] * parts[:, :, d]).reshape(8 * COLS, LANES).astype(jnp.bfloat16)
                for parts in (plain_parts, swapped_parts)
            ],
            axis=1,
        )
        part = jnp.dot(products, col_ref[d], preferred_element_type=jnp.float32)
        columns = part if columns is None else columns + part
    columns = (columns[:, :LANES] + columns[:, LANES:]).reshape(ORI_MAX * PART_DEV, 8, LANES)
    summed = jnp.sum(columns * row_ref[...][None], axis=1)
    folded = (summed + pltpu.roll(summed, TRANS, 1)).reshape(ORI_MAX // 2, 2, PART_DEV, LANES)
    left = lax.broadcasted_iota(jnp.int32, (ORI_MAX // 2, PART_DEV, LANES), 2) < TRANS
    total = jnp.where(left, folded[:, 0], folded[:, 1])

    @pl.when(pl.program_id(0) == 0)
    def _():
        out_ref[...] = total

    @pl.when(pl.program_id(0) > 0)
    def _():
        out_ref[...] += total


def score(order, buffer, weighted, col_phase, row_phase):
    return pl.pallas_call(
        score_kernel,
        grid_spec=pltpu.PrefetchScalarGridSpec(
            num_scalar_prefetch=1,
            grid=(N_GRP,),
            in_specs=[
                pl.BlockSpec(
                    (32, None, 4 * CAP, LANES), lambda i, order: (0, order[i], 0, 0)
                ),
            ]
            + [pl.BlockSpec((PARTICLE_ROWS + EXTRA_ROWS, LANES), lambda i, order: (0, 0))] * 4
            + [
                pl.BlockSpec((8, 2 * LANES, 2 * LANES), lambda i, order: (0, 0, 0)),
                pl.BlockSpec((None, 8, LANES), lambda i, order: (order[i], 0, 0)),
            ],
            out_specs=pl.BlockSpec(
                (ORI_MAX // 2, PART_DEV, LANES), lambda i, order: (0, 0, 0)
            ),
            scratch_shapes=[
                pltpu.VMEM((TAKES, LANES), jnp.float32),
                pltpu.VMEM((PARTICLE_ROWS + EXTRA_ROWS, LANES), jnp.bfloat16),
            ],
        ),
        out_shape=jax.ShapeDtypeStruct((ORI_MAX // 2, PART_DEV, LANES), jnp.float32),
        compiler_params=pltpu.CompilerParams(vmem_limit_bytes=VMEM_BYTES),
        cost_estimate=pl.CostEstimate(flops=8 << 30, bytes_accessed=4 << 20, transcendentals=0),
    )(order, buffer, *weighted, col_phase, row_phase)


def exchange(values, axes):
    return lax.all_to_all(values, axes, split_axis=0, concat_axis=0, tiled=True)


def own_part(table, axis):
    return lax.dynamic_index_in_dim(jnp.asarray(table), lax.axis_index(axis), 0, keepdims=False)


def shards(pencils, send_map, interp_index, interp_frac, ori_count, spectra, class_ids, ctf_table):
    here = lax.axis_index("x")
    turn = jnp.arange(4, dtype=jnp.int32)
    table = exchange(fourier(pencils, jnp.asarray(fourier_tables())), SLAB_AXES)

    wanted = jnp.maximum(send_map[0, 0], 0)
    place = ((wanted & 1) << 8) | (wanted & (NF - 2)) | (wanted >> 8)
    place = place.astype(jnp.float32).reshape(4, 4, 8, CAP).transpose(1, 0, 2, 3)
    place = place.reshape(4, 4, LANES)
    maps = [place] + [
        lax.ppermute(place, "x", [((i + k) % 4, i) for i in range(4)]) for k in range(1, 4)
    ]
    maps = lax.all_gather(jnp.stack(maps), "h", axis=0)
    maps = lax.dynamic_index_in_dim(maps, lax.axis_index("h"), 2, keepdims=False)
    outgoing = pick((here + turn) % 4, maps, table)

    slot = interp_index.reshape(2, TAKES)
    slab = slot >> 4
    source = ((slab >> 5) << 3) | (slab & 7)
    slot = ((source << 6) | (((slab >> 3) & 3) << 4) | (slot & 15)).astype(jnp.float32)
    taps = jnp.concatenate([slot.reshape(8, LANES), interp_frac.reshape(4, LANES)], axis=0)
    weighted = weigh(class_ids, spectra, ctf_table, taps)
    outgoing = outgoing.reshape(32 * N_GRP * 4 * CAP, LANES)
    buffer = exchange(outgoing, ROW_AXES).reshape(32, N_GRP, 4 * CAP, LANES)
    groups = [lax.dynamic_index_in_dim(weighted, here, 0, keepdims=False)]
    for k in range(1, 4):
        block = lax.dynamic_index_in_dim(weighted, (here - k) % 4, 0, keepdims=False)
        groups.append(lax.ppermute(block, "x", [((i + k) % 4, i) for i in range(4)]))
    partial = score(
        (here + turn) % 4,
        buffer,
        groups,
        own_part(column_table(), "x"),
        jnp.asarray(row_table()),
    )
    total = jnp.sum(exchange(partial, "x"), axis=0)
    orient = 2 * here + jnp.arange(LANES, dtype=jnp.int32) // TRANS
    return jnp.where(orient[None, :] < ori_count[0], total, 0.0)


def solution(mesh):
    fine = Mesh(mesh.devices.reshape(4, 4, 4, 2, 4), SLAB_AXES + ("x",))
    return jax.shard_map(
        shards,
        mesh=fine,
        in_specs=(
            P(SLAB_AXES, "x", None),
            P(SLAB_AXES, "x", None, None),
            P(None, SLAB_AXES, None, "x"),
            P(SLAB_AXES, None, "x"),
            P(SLAB_AXES),
            P(SLAB_AXES, "x", None),
            P(SLAB_AXES),
            P(None, "x", None),
        ),
        out_specs=P(SLAB_AXES, "x"),
        check_vma=False,
    )
```

```python
import math

import jax
import jax.numpy as jnp
import ml_dtypes
import numpy as np
from jax import lax
from jax.experimental import pallas as pl
from jax.experimental.pallas import tpu as pltpu
from jax.sharding import Mesh
from jax.sharding import PartitionSpec as P

NF = 256
CAP = 16
ORI_MAX = 8
TSIDE = 8
PART_DEV = 8
TRANS = 64
N_GRP = 4
COLS = NF // N_GRP
LANES = 2 * COLS
SLAB_ROWS = 512
SLOTS = 2048
TAKES = ORI_MAX * COLS
PARTICLE_ROWS = PART_DEV * COLS
MIX_STEP = 256
EXTRA_ROWS = 32
VMEM_BYTES = 48 * 1024 * 1024
SLAB_AXES = ("y", "h", "l", "c")
ROW_AXES = ("y", "l", "c")


def split_bf16(values):
    high = values.astype(ml_dtypes.bfloat16)
    low = (values - high.astype(np.float64)).astype(ml_dtypes.bfloat16)
    return high, low


def fourier_tables():
    index = np.arange(NF)
    kz = index.reshape(4, 4, 8, 2).transpose(0, 2, 3, 1).reshape(NF)
    angle = 2.0 * math.pi / NF * ((kz[:, None] * index[None, :]) % NF)
    table = np.concatenate([np.cos(angle), np.sin(angle)], axis=1) / math.sqrt(NF)
    return np.stack(split_bf16(table))


def column_table():
    t = np.arange(TRANS)
    a = t // TSIDE - TSIDE // 2
    b = t % TSIDE - TSIDE // 2
    v = np.arange(NF).reshape(N_GRP, 1, COLS, 1)
    d = np.arange(8).reshape(1, 8, 1, 1)
    angle = -2.0 * math.pi / NF * ((b * v + 8 * a * d) % NF)
    fr = np.cos(angle) / NF
    fi = np.sin(angle) / NF
    with_er = np.concatenate([fr, fr, -fi, fi], axis=2)
    with_ei = np.concatenate([-fi, -fi, -fr, fr], axis=2)
    high, low = split_bf16(np.concatenate([with_er, with_ei], axis=3))
    return np.concatenate([high, low], axis=3)


def row_table():
    a = np.arange(TRANS) // TSIDE - TSIDE // 2
    u = np.arange(NF).reshape(N_GRP, COLS)[:, :8]
    angle = -2.0 * math.pi / NF * ((a * u[:, :, None]) % NF)
    return np.concatenate([np.cos(angle), np.sin(angle)], axis=2).astype(np.float32)


def down_rows(row):
    return jnp.broadcast_to(row, (LANES, LANES)).T


def fourier_kernel(x_ref, table_ref, out_ref, wide):
    contract = (((1,), (1,)), ((), ()))
    for ky in range(2):
        lines = x_ref[ky]
        turned = jnp.concatenate([lines[:, NF:], -lines[:, :NF]], axis=1)
        both = jnp.concatenate([lines, turned], axis=0)
        high = both.astype(jnp.bfloat16)
        low = (both - high.astype(jnp.float32)).astype(jnp.bfloat16)

        def product(table, part):
            return lax.dot_general(table, part, contract, preferred_element_type=jnp.float32)

        result = (product(table_ref[0], low) + product(table_ref[1], high)) + product(
            table_ref[0], high
        )
        wide[pl.ds(ky, NF, stride=2), :] = result
    rest = 2 * NF // 4
    for y in range(4):
        block = wide[y * rest : (y + 1) * rest, :].astype(jnp.bfloat16)
        for h in range(4):
            out_ref[(y * 4 + h) * rest : (y * 4 + h + 1) * rest, :] = block


def fourier(pencils, table):
    return pl.pallas_call(
        fourier_kernel,
        out_shape=jax.ShapeDtypeStruct((8 * NF, LANES), jnp.bfloat16),
        scratch_shapes=[pltpu.VMEM((2 * NF, LANES), jnp.float32)],
        compiler_params=pltpu.CompilerParams(vmem_limit_bytes=VMEM_BYTES),
        cost_estimate=pl.CostEstimate(
            flops=6 * NF * NF * 2 * NF, bytes_accessed=1 << 20, transcendentals=0
        ),
    )(pencils, table)


def weigh_kernel(class_ref, spectra_ref, ctf_ref, taps_ref, out_ref):
    for particle in range(PART_DEV):
        factor = ctf_ref[class_ref[particle]].astype(jnp.float32)
        lines = spectra_ref[particle].astype(jnp.float32)
        real = lines[:, :NF] * factor
        imag = lines[:, NF:] * factor
        for part in range(N_GRP):
            span = slice(part * COLS, (part + 1) * COLS)
            out_ref[part, particle * COLS : (particle + 1) * COLS, :] = jnp.concatenate(
                [real[:, span], imag[:, span]], axis=1
            ).astype(jnp.bfloat16)
    taps = taps_ref[...]
    place = taps[:8]
    place_high = jnp.floor(place * (1.0 / 16.0))
    place_low = place - 16.0 * place_high
    frac = taps[8:12]
    first = frac.astype(jnp.bfloat16).astype(jnp.float32)
    second = (frac - first).astype(jnp.bfloat16).astype(jnp.float32)
    third = frac - first - second
    extra = jnp.concatenate(
        [place_high, place_low, first, second, third, jnp.zeros_like(frac)], axis=0
    ).astype(jnp.bfloat16)
    for part in range(N_GRP):
        out_ref[part, PARTICLE_ROWS:, :] = extra


def weigh(class_ids, spectra, ctf_table, taps):
    vmem = pl.BlockSpec(memory_space=pltpu.VMEM)
    return pl.pallas_call(
        weigh_kernel,
        in_specs=[pl.BlockSpec(memory_space=pltpu.SMEM)] + [vmem] * 3,
        out_specs=vmem,
        out_shape=jax.ShapeDtypeStruct((N_GRP, PARTICLE_ROWS + EXTRA_ROWS, LANES), jnp.bfloat16),
        compiler_params=pltpu.CompilerParams(vmem_limit_bytes=VMEM_BYTES),
        cost_estimate=pl.CostEstimate(flops=1 << 20, bytes_accessed=2 << 20, transcendentals=0),
    )(class_ids, spectra, ctf_table, taps)


def pick_kernel(order_ref, place_ref, table_ref, out_ref, wide, slabs, hits):
    del order_ref

    @pl.when(pl.program_id(0) == 0)
    def _():
        wide[...] = table_ref[...].astype(jnp.float32)
        for slab in range(4):
            for ky in range(2):
                slabs[slab, :, ky * LANES : (ky + 1) * LANES] = wide[
                    pl.ds(2 * slab + ky, NF, stride=8), :
                ].astype(jnp.bfloat16)

    lane = lax.broadcasted_iota(jnp.int32, (LANES, LANES), 1).astype(jnp.float32)
    for slab in range(4):
        later = []
        for row in range(4):
            column = down_rows(place_ref[slab, row : row + 1, :])
            later.append(column >= float(NF))
            ahead = jnp.where(later[-1], column - float(NF), column) - lane
            for first in range(0, NF, LANES):
                hits[row * LANES : (row + 1) * LANES, first : first + LANES] = jnp.where(
                    ahead == float(first), 1.0, 0.0
                ).astype(jnp.bfloat16)
        taken = jnp.dot(hits[...], slabs[slab], preferred_element_type=jnp.float32)
        for row in range(4):
            span = taken[row * LANES : (row + 1) * LANES]
            chosen = jnp.where(later[row], span[:, LANES:], span[:, :LANES])
            out_ref[row * 8 : (row + 1) * 8, slab, :, :] = chosen.astype(jnp.bfloat16).reshape(
                8, CAP, LANES
            )


def pick(order, place, table):
    return pl.pallas_call(
        pick_kernel,
        grid_spec=pltpu.PrefetchScalarGridSpec(
            num_scalar_prefetch=1,
            grid=(N_GRP,),
            in_specs=[
                pl.BlockSpec((4, None, 4, LANES), lambda i, order: (0, i, 0, 0)),
                pl.BlockSpec(memory_space=pltpu.VMEM),
            ],
            out_specs=pl.BlockSpec(
                (32, None, 4, CAP, LANES), lambda i, order: (0, order[i], 0, 0, 0)
            ),
            scratch_shapes=[
                pltpu.VMEM((4 * SLAB_ROWS, LANES), jnp.float32),
                pltpu.VMEM((4, NF, 2 * LANES), jnp.bfloat16),
                pltpu.VMEM((SLAB_ROWS, NF), jnp.bfloat16),
            ],
        ),
        out_shape=pltpu.HBM((32, N_GRP, 4, CAP, LANES), jnp.bfloat16),
        compiler_params=pltpu.CompilerParams(vmem_limit_bytes=VMEM_BYTES),
        cost_estimate=pl.CostEstimate(
            flops=16 * SLOTS * SLAB_ROWS * LANES, bytes_accessed=4 << 20, transcendentals=0
        ),
    )(order, place, table)


def score_kernel(order_ref, buffer_ref, w0, w1, w2, w3, col_ref, row_ref, out_ref, slices, weighted_ref):
    for at, source in enumerate((w0, w1, w2, w3)):

        @pl.when(pl.program_id(0) == at)
        def _(source=source):
            weighted_ref[...] = source[...]

    extra = weighted_ref[PARTICLE_ROWS:, :].astype(jnp.float32)
    place = 16.0 * extra[:8] + extra[8:16]
    frac = extra[16:20] + extra[20:24] + extra[24:28]
    lane = lax.broadcasted_iota(jnp.int32, (LANES, LANES), 1).astype(jnp.float32)
    takes = []
    for row in range(4):
        share = down_rows(frac[row : row + 1])
        takes.append(
            (
                down_rows(place[row : row + 1]) - lane,
                1.0 - share,
                down_rows(place[row + 4 : row + 5]) - lane,
                share,
            )
        )
    rows = buffer_ref[:, order_ref[pl.program_id(0)]].reshape(SLOTS, LANES)
    mixed = None
    for start in range(0, SLOTS, MIX_STEP):
        blocks = [
            jnp.concatenate(
                [
                    (
                        jnp.where(far == float(first), rest, 0.0)
                        + jnp.where(far_next == float(first), share, 0.0)
                    ).astype(jnp.bfloat16)
                    for first in range(start, start + MIX_STEP, LANES)
                ],
                axis=1,
            )
            for far, rest, far_next, share in takes
        ]
        part = jnp.dot(
            jnp.concatenate(blocks, axis=0),
            rows[start : start + MIX_STEP],
            preferred_element_type=jnp.float32,
        )
        mixed = part if mixed is None else mixed + part
    slices[...] = mixed
    plain = slices[...]
    plain_parts = plain.reshape(ORI_MAX, 1, 8, 8, LANES)
    swapped_parts = pltpu.roll(plain, COLS, 1).reshape(ORI_MAX, 1, 8, 8, LANES)
    weight = weighted_ref[:PARTICLE_ROWS, :].astype(jnp.float32)
    weight = weight.reshape(1, PART_DEV, 8, 8, LANES)
    columns = None
    for d in range(8):
        products = jnp.concatenate(
            [
                (weight[:, :, d] * parts[:, :, d]).reshape(8 * COLS, LANES).astype(jnp.bfloat16)
                for parts in (plain_parts, swapped_parts)
            ],
            axis=1,
        )
        part = jnp.dot(products, col_ref[d], preferred_element_type=jnp.float32)
        columns = part if columns is None else columns + part
    columns = (columns[:, :LANES] + columns[:, LANES:]).reshape(ORI_MAX * PART_DEV, 8, LANES)
    summed = jnp.sum(columns * row_ref[...][None], axis=1)
    folded = (summed + pltpu.roll(summed, TRANS, 1)).reshape(ORI_MAX // 2, 2, PART_DEV, LANES)
    left = lax.broadcasted_iota(jnp.int32, (ORI_MAX // 2, PART_DEV, LANES), 2) < TRANS
    total = jnp.where(left, folded[:, 0], folded[:, 1])

    @pl.when(pl.program_id(0) == 0)
    def _():
        out_ref[...] = total

    @pl.when(pl.program_id(0) > 0)
    def _():
        out_ref[...] += total


def score(order, buffer, weighted, col_phase, row_phase):
    return pl.pallas_call(
        score_kernel,
        grid_spec=pltpu.PrefetchScalarGridSpec(
            num_scalar_prefetch=1,
            grid=(N_GRP,),
            in_specs=[
                pl.BlockSpec(memory_space=pltpu.VMEM),
            ]
            + [pl.BlockSpec(memory_space=pltpu.VMEM)] * 4
            + [
                pl.BlockSpec(memory_space=pltpu.VMEM),
                pl.BlockSpec((None, 8, LANES), lambda i, order: (order[i], 0, 0)),
            ],
            out_specs=pl.BlockSpec(
                (ORI_MAX // 2, PART_DEV, LANES), lambda i, order: (0, 0, 0)
            ),
            scratch_shapes=[
                pltpu.VMEM((TAKES, LANES), jnp.float32),
                pltpu.VMEM((PARTICLE_ROWS + EXTRA_ROWS, LANES), jnp.bfloat16),
            ],
        ),
        out_shape=jax.ShapeDtypeStruct((ORI_MAX // 2, PART_DEV, LANES), jnp.float32),
        compiler_params=pltpu.CompilerParams(vmem_limit_bytes=VMEM_BYTES),
        cost_estimate=pl.CostEstimate(flops=8 << 30, bytes_accessed=4 << 20, transcendentals=0),
    )(order, buffer, *weighted, col_phase, row_phase)


def exchange(values, axes):
    return lax.all_to_all(values, axes, split_axis=0, concat_axis=0, tiled=True)


def own_part(table, axis):
    return lax.dynamic_index_in_dim(jnp.asarray(table), lax.axis_index(axis), 0, keepdims=False)


def shards(pencils, send_map, interp_index, interp_frac, ori_count, spectra, class_ids, ctf_table):
    here = lax.axis_index("x")
    turn = jnp.arange(4, dtype=jnp.int32)
    table = exchange(fourier(pencils, jnp.asarray(fourier_tables())), SLAB_AXES)

    wanted = jnp.maximum(send_map[0, 0], 0)
    place = ((wanted & 1) << 8) | (wanted & (NF - 2)) | (wanted >> 8)
    place = place.astype(jnp.float32).reshape(4, 4, 8, CAP).transpose(1, 0, 2, 3)
    place = place.reshape(4, 4, LANES)
    maps = [place] + [
        lax.ppermute(place, "x", [((i + k) % 4, i) for i in range(4)]) for k in range(1, 4)
    ]
    maps = lax.all_gather(jnp.stack(maps), "h", axis=0)
    maps = lax.dynamic_index_in_dim(maps, lax.axis_index("h"), 2, keepdims=False)
    outgoing = pick((here + turn) % 4, maps, table)

    slot = interp_index.reshape(2, TAKES)
    slab = slot >> 4
    source = ((slab >> 5) << 3) | (slab & 7)
    slot = ((source << 6) | (((slab >> 3) & 3) << 4) | (slot & 15)).astype(jnp.float32)
    taps = jnp.concatenate([slot.reshape(8, LANES), interp_frac.reshape(4, LANES)], axis=0)
    weighted = weigh(class_ids, spectra, ctf_table, taps)
    outgoing = outgoing.reshape(32 * N_GRP * 4 * CAP, LANES)
    buffer = exchange(outgoing, ROW_AXES).reshape(32, N_GRP, 4 * CAP, LANES)
    groups = [lax.dynamic_index_in_dim(weighted, here, 0, keepdims=False)]
    for k in range(1, 4):
        block = lax.dynamic_index_in_dim(weighted, (here - k) % 4, 0, keepdims=False)
        groups.append(lax.ppermute(block, "x", [((i + k) % 4, i) for i in range(4)]))
    partial = score(
        (here + turn) % 4,
        buffer,
        groups,
        own_part(column_table(), "x"),
        jnp.asarray(row_table()),
    )
    total = jnp.sum(exchange(partial, "x"), axis=0)
    orient = 2 * here + jnp.arange(LANES, dtype=jnp.int32) // TRANS
    return jnp.where(orient[None, :] < ori_count[0], total, 0.0)


def solution(mesh):
    fine = Mesh(mesh.devices.reshape(4, 4, 4, 2, 4), SLAB_AXES + ("x",))
    return jax.shard_map(
        shards,
        mesh=fine,
        in_specs=(
            P(SLAB_AXES, "x", None),
            P(SLAB_AXES, "x", None, None),
            P(None, SLAB_AXES, None, "x"),
            P(SLAB_AXES, None, "x"),
            P(SLAB_AXES),
            P(SLAB_AXES, "x", None),
            P(SLAB_AXES),
            P(None, "x", None),
        ),
        out_specs=P(SLAB_AXES, "x"),
        check_vma=False,
    )
```

```python
import math

import jax
import jax.numpy as jnp
import ml_dtypes
import numpy as np
from jax import lax
from jax.experimental import pallas as pl
from jax.experimental.pallas import tpu as pltpu
from jax.sharding import Mesh
from jax.sharding import PartitionSpec as P

NF = 256
CAP = 16
ORI_MAX = 8
TSIDE = 8
PART_DEV = 8
TRANS = 64
N_GRP = 4
COLS = NF // N_GRP
LANES = 2 * COLS
SLAB_ROWS = 512
SLOTS = 2048
TAKES = ORI_MAX * COLS
PARTICLE_ROWS = PART_DEV * COLS
MIX_STEP = 256
EXTRA_ROWS = 32
VMEM_BYTES = 48 * 1024 * 1024
SLAB_AXES = ("y", "h", "l", "c")
ROW_AXES = ("y", "l", "c")


def split_bf16(values):
    high = values.astype(ml_dtypes.bfloat16)
    low = (values - high.astype(np.float64)).astype(ml_dtypes.bfloat16)
    return high, low


def fourier_tables():
    index = np.arange(NF)
    kz = index.reshape(4, 4, 8, 2).transpose(0, 2, 3, 1).reshape(NF)
    angle = 2.0 * math.pi / NF * ((kz[:, None] * index[None, :]) % NF)
    table = np.concatenate([np.cos(angle), np.sin(angle)], axis=1) / math.sqrt(NF)
    return np.stack(split_bf16(table))


def column_table():
    t = np.arange(TRANS)
    a = t // TSIDE - TSIDE // 2
    b = t % TSIDE - TSIDE // 2
    v = np.arange(NF).reshape(N_GRP, 1, COLS, 1)
    d = np.arange(8).reshape(1, 8, 1, 1)
    angle = -2.0 * math.pi / NF * ((b * v + 8 * a * d) % NF)
    fr = np.cos(angle) / NF
    fi = np.sin(angle) / NF
    with_er = np.concatenate([fr, fr, -fi, fi], axis=2)
    with_ei = np.concatenate([-fi, -fi, -fr, fr], axis=2)
    high, low = split_bf16(np.concatenate([with_er, with_ei], axis=3))
    return np.concatenate([high, low], axis=3)


def row_table():
    a = np.arange(TRANS) // TSIDE - TSIDE // 2
    u = np.arange(NF).reshape(N_GRP, COLS)[:, :8]
    angle = -2.0 * math.pi / NF * ((a * u[:, :, None]) % NF)
    return np.concatenate([np.cos(angle), np.sin(angle)], axis=2).astype(np.float32)


def down_rows(row):
    return jnp.broadcast_to(row, (LANES, LANES)).T


def fourier_kernel(x_ref, table_ref, out_ref, wide):
    contract = (((1,), (1,)), ((), ()))
    for ky in range(2):
        lines = x_ref[ky]
        turned = jnp.concatenate([lines[:, NF:], -lines[:, :NF]], axis=1)
        both = jnp.concatenate([lines, turned], axis=0)
        high = both.astype(jnp.bfloat16)
        low = (both - high.astype(jnp.float32)).astype(jnp.bfloat16)

        def product(table, part):
            return lax.dot_general(table, part, contract, preferred_element_type=jnp.float32)

        result = (product(table_ref[0], low) + product(table_ref[1], high)) + product(
            table_ref[0], high
        )
        wide[pl.ds(ky, NF, stride=2), :] = result
    rest = 2 * NF // 4
    for y in range(4):
        block = wide[y * rest : (y + 1) * rest, :].astype(jnp.bfloat16)
        for h in range(4):
            out_ref[(y * 4 + h) * rest : (y * 4 + h + 1) * rest, :] = block


def fourier(pencils, table):
    return pl.pallas_call(
        fourier_kernel,
        out_shape=jax.ShapeDtypeStruct((8 * NF, LANES), jnp.bfloat16),
        scratch_shapes=[pltpu.VMEM((2 * NF, LANES), jnp.float32)],
        compiler_params=pltpu.CompilerParams(vmem_limit_bytes=VMEM_BYTES),
        cost_estimate=pl.CostEstimate(
            flops=6 * NF * NF * 2 * NF, bytes_accessed=1 << 20, transcendentals=0
        ),
    )(pencils, table)


def weigh_kernel(class_ref, spectra_ref, ctf_ref, taps_ref, out_ref):
    for particle in range(PART_DEV):
        factor = ctf_ref[class_ref[particle]].astype(jnp.float32)
        lines = spectra_ref[particle].astype(jnp.float32)
        real = lines[:, :NF] * factor
        imag = lines[:, NF:] * factor
        for part in range(N_GRP):
            span = slice(part * COLS, (part + 1) * COLS)
            out_ref[part, particle * COLS : (particle + 1) * COLS, :] = jnp.concatenate(
                [real[:, span], imag[:, span]], axis=1
            ).astype(jnp.bfloat16)
    taps = taps_ref[...]
    place = taps[:8]
    place_high = jnp.floor(place * (1.0 / 16.0))
    place_low = place - 16.0 * place_high
    frac = taps[8:12]
    first = frac.astype(jnp.bfloat16).astype(jnp.float32)
    second = (frac - first).astype(jnp.bfloat16).astype(jnp.float32)
    third = frac - first - second
    extra = jnp.concatenate(
        [place_high, place_low, first, second, third, jnp.zeros_like(frac)], axis=0
    ).astype(jnp.bfloat16)
    for part in range(N_GRP):
        out_ref[part, PARTICLE_ROWS:, :] = extra


def weigh(class_ids, spectra, ctf_table, taps):
    vmem = pl.BlockSpec(memory_space=pltpu.VMEM)
    return pl.pallas_call(
        weigh_kernel,
        in_specs=[pl.BlockSpec(memory_space=pltpu.SMEM)] + [vmem] * 3,
        out_specs=vmem,
        out_shape=jax.ShapeDtypeStruct((N_GRP, PARTICLE_ROWS + EXTRA_ROWS, LANES), jnp.bfloat16),
        compiler_params=pltpu.CompilerParams(vmem_limit_bytes=VMEM_BYTES),
        cost_estimate=pl.CostEstimate(flops=1 << 20, bytes_accessed=2 << 20, transcendentals=0),
    )(class_ids, spectra, ctf_table, taps)


def pick_kernel(order_ref, place_ref, table_ref, out_ref, wide, slabs, hits):
    del order_ref

    @pl.when(pl.program_id(0) == 0)
    def _():
        wide[...] = table_ref[...].astype(jnp.float32)
        for slab in range(4):
            for ky in range(2):
                slabs[slab, :, ky * LANES : (ky + 1) * LANES] = wide[
                    pl.ds(2 * slab + ky, NF, stride=8), :
                ].astype(jnp.bfloat16)

    lane = lax.broadcasted_iota(jnp.int32, (LANES, LANES), 1).astype(jnp.float32)
    for slab in range(4):
        later = []
        for row in range(4):
            column = down_rows(place_ref[slab, row : row + 1, :])
            later.append(column >= float(NF))
            ahead = jnp.where(later[-1], column - float(NF), column) - lane
            for first in range(0, NF, LANES):
                hits[row * LANES : (row + 1) * LANES, first : first + LANES] = jnp.where(
                    ahead == float(first), 1.0, 0.0
                ).astype(jnp.bfloat16)
        taken = jnp.dot(hits[...], slabs[slab], preferred_element_type=jnp.float32)
        for row in range(4):
            span = taken[row * LANES : (row + 1) * LANES]
            chosen = jnp.where(later[row], span[:, LANES:], span[:, :LANES])
            out_ref[row * 8 : (row + 1) * 8, slab, :, :] = chosen.astype(jnp.bfloat16).reshape(
                8, CAP, LANES
            )


def pick(order, place, table):
    return pl.pallas_call(
        pick_kernel,
        grid_spec=pltpu.PrefetchScalarGridSpec(
            num_scalar_prefetch=1,
            grid=(N_GRP,),
            in_specs=[
                pl.BlockSpec((4, None, 4, LANES), lambda i, order: (0, i, 0, 0)),
                pl.BlockSpec(memory_space=pltpu.VMEM),
            ],
            out_specs=pl.BlockSpec(
                (32, None, 4, CAP, LANES), lambda i, order: (0, order[i], 0, 0, 0)
            ),
            scratch_shapes=[
                pltpu.VMEM((4 * SLAB_ROWS, LANES), jnp.float32),
                pltpu.VMEM((4, NF, 2 * LANES), jnp.bfloat16),
                pltpu.VMEM((SLAB_ROWS, NF), jnp.bfloat16),
            ],
        ),
        out_shape=pltpu.HBM((32, N_GRP, 4, CAP, LANES), jnp.bfloat16),
        compiler_params=pltpu.CompilerParams(vmem_limit_bytes=VMEM_BYTES),
        cost_estimate=pl.CostEstimate(
            flops=16 * SLOTS * SLAB_ROWS * LANES, bytes_accessed=4 << 20, transcendentals=0
        ),
    )(order, place, table)


def score_kernel(order_ref, buffer_ref, w0, w1, w2, w3, col_ref, row_ref, out_ref, slices, weighted_ref):
    for at, source in enumerate((w0, w1, w2, w3)):

        @pl.when(pl.program_id(0) == at)
        def _(source=source):
            weighted_ref[...] = source[...]

    extra = weighted_ref[PARTICLE_ROWS:, :].astype(jnp.float32)
    place = 16.0 * extra[:8] + extra[8:16]
    frac = extra[16:20] + extra[20:24] + extra[24:28]
    lane = lax.broadcasted_iota(jnp.int32, (LANES, LANES), 1).astype(jnp.float32)
    takes = []
    for row in range(4):
        share = down_rows(frac[row : row + 1])
        takes.append(
            (
                down_rows(place[row : row + 1]) - lane,
                1.0 - share,
                down_rows(place[row + 4 : row + 5]) - lane,
                share,
            )
        )
    rows = buffer_ref[:, order_ref[pl.program_id(0)]].reshape(SLOTS, LANES)
    mixed = None
    for start in range(0, SLOTS, MIX_STEP):
        blocks = [
            jnp.concatenate(
                [
                    (
                        jnp.where(far == float(first), rest, 0.0)
                        + jnp.where(far_next == float(first), share, 0.0)
                    ).astype(jnp.bfloat16)
                    for first in range(start, start + MIX_STEP, LANES)
                ],
                axis=1,
            )
            for far, rest, far_next, share in takes
        ]
        part = jnp.dot(
            jnp.concatenate(blocks, axis=0),
            rows[start : start + MIX_STEP],
            preferred_element_type=jnp.float32,
        )
        mixed = part if mixed is None else mixed + part
    slices[...] = mixed
    plain = slices[...]
    plain_parts = plain.reshape(ORI_MAX, 1, 8, 8, LANES)
    swapped_parts = pltpu.roll(plain, COLS, 1).reshape(ORI_MAX, 1, 8, 8, LANES)
    weight = weighted_ref[:PARTICLE_ROWS, :].astype(jnp.float32)
    weight = weight.reshape(1, PART_DEV, 8, 8, LANES)
    columns = None
    for d in range(8):
        products = jnp.concatenate(
            [
                (weight[:, :, d] * parts[:, :, d]).reshape(8 * COLS, LANES).astype(jnp.bfloat16)
                for parts in (plain_parts, swapped_parts)
            ],
            axis=1,
        )
        part = jnp.dot(products, col_ref[d], preferred_element_type=jnp.float32)
        columns = part if columns is None else columns + part
    columns = (columns[:, :LANES] + columns[:, LANES:]).reshape(ORI_MAX * PART_DEV, 8, LANES)
    summed = jnp.sum(columns * row_ref[...][None], axis=1)
    folded = (summed + pltpu.roll(summed, TRANS, 1)).reshape(ORI_MAX // 2, 2, PART_DEV, LANES)
    left = lax.broadcasted_iota(jnp.int32, (ORI_MAX // 2, PART_DEV, LANES), 2) < TRANS
    total = jnp.where(left, folded[:, 0], folded[:, 1])

    @pl.when(pl.program_id(0) == 0)
    def _():
        out_ref[...] = total

    @pl.when(pl.program_id(0) > 0)
    def _():
        out_ref[...] += total


def score(order, buffer, weighted, col_phase, row_phase):
    return pl.pallas_call(
        score_kernel,
        grid_spec=pltpu.PrefetchScalarGridSpec(
            num_scalar_prefetch=1,
            grid=(N_GRP,),
            in_specs=[
                pl.BlockSpec(memory_space=pltpu.VMEM),
            ]
            + [pl.BlockSpec(memory_space=pltpu.VMEM)] * 4
            + [
                pl.BlockSpec(memory_space=pltpu.VMEM),
                pl.BlockSpec((None, 8, LANES), lambda i, order: (order[i], 0, 0)),
            ],
            out_specs=pl.BlockSpec(
                (ORI_MAX // 2, PART_DEV, LANES), lambda i, order: (0, 0, 0)
            ),
            scratch_shapes=[
                pltpu.VMEM((TAKES, LANES), jnp.float32),
                pltpu.VMEM((PARTICLE_ROWS + EXTRA_ROWS, LANES), jnp.bfloat16),
            ],
        ),
        out_shape=jax.ShapeDtypeStruct((ORI_MAX // 2, PART_DEV, LANES), jnp.float32),
        compiler_params=pltpu.CompilerParams(vmem_limit_bytes=VMEM_BYTES),
        cost_estimate=pl.CostEstimate(flops=8 << 30, bytes_accessed=4 << 20, transcendentals=0),
    )(order, buffer, *weighted, col_phase, row_phase)


def exchange(values, axes):
    return lax.all_to_all(values, axes, split_axis=0, concat_axis=0, tiled=True)


def own_part(table, axis):
    return lax.dynamic_index_in_dim(jnp.asarray(table), lax.axis_index(axis), 0, keepdims=False)


def shards(pencils, send_map, interp_index, interp_frac, ori_count, spectra, class_ids, ctf_table):
    here = lax.axis_index("x")
    turn = jnp.arange(4, dtype=jnp.int32)
    table = exchange(fourier(pencils, jnp.asarray(fourier_tables())), SLAB_AXES)

    wanted = jnp.maximum(send_map[0, 0], 0)
    place = ((wanted & 1) << 8) | (wanted & (NF - 2)) | (wanted >> 8)
    place = place.astype(jnp.float32).reshape(4, 4, 8, CAP).transpose(1, 0, 2, 3)
    place = place.reshape(4, 4, LANES)
    maps = lax.all_gather(lax.all_gather(place, "x", axis=0), "h", axis=0)
    maps = lax.dynamic_index_in_dim(maps, lax.axis_index("h"), 2, keepdims=False)
    outgoing = pick(turn, maps, table)

    slot = interp_index.reshape(2, TAKES)
    slab = slot >> 4
    source = ((slab >> 5) << 3) | (slab & 7)
    slot = ((source << 6) | (((slab >> 3) & 3) << 4) | (slot & 15)).astype(jnp.float32)
    taps = jnp.concatenate([slot.reshape(8, LANES), interp_frac.reshape(4, LANES)], axis=0)
    weighted = weigh(class_ids, spectra, ctf_table, taps)
    outgoing = outgoing.reshape(32 * N_GRP * 4 * CAP, LANES)
    buffer = exchange(outgoing, ROW_AXES).reshape(32, N_GRP, 4 * CAP, LANES)
    groups = [lax.dynamic_index_in_dim(weighted, here, 0, keepdims=False)]
    for k in range(1, 4):
        block = lax.dynamic_index_in_dim(weighted, (here - k) % 4, 0, keepdims=False)
        groups.append(lax.ppermute(block, "x", [((i + k) % 4, i) for i in range(4)]))
    partial = score(
        (here + turn) % 4,
        buffer,
        groups,
        own_part(column_table(), "x"),
        jnp.asarray(row_table()),
    )
    total = jnp.sum(exchange(partial, "x"), axis=0)
    orient = 2 * here + jnp.arange(LANES, dtype=jnp.int32) // TRANS
    return jnp.where(orient[None, :] < ori_count[0], total, 0.0)


def solution(mesh):
    fine = Mesh(mesh.devices.reshape(4, 4, 4, 2, 4), SLAB_AXES + ("x",))
    return jax.shard_map(
        shards,
        mesh=fine,
        in_specs=(
            P(SLAB_AXES, "x", None),
            P(SLAB_AXES, "x", None, None),
            P(None, SLAB_AXES, None, "x"),
            P(SLAB_AXES, None, "x"),
            P(SLAB_AXES),
            P(SLAB_AXES, "x", None),
            P(SLAB_AXES),
            P(None, "x", None),
        ),
        out_specs=P(SLAB_AXES, "x"),
        check_vma=False,
    )
```
